256 devices in a mesh: patch: 64 (over x, y_hi, z), head: 4 (over y_lo, core).
Axes of the slice: x: 4, y: 4 (y_hi: 2, y_lo: 2; y = y_hi * 2 + y_lo), z: 8, core: 2. Of those that a mesh axis runs over, the one named last changes fastest.
Arguments:
- image_tokens: bfloat16 [16384, 3072], P('patch'), may hold values from -6 to 6
- refresh: int32 [128], P('patch'), may hold values 0 or 1
- qkv_weight: bfloat16 [3072, 3, 1536], P(None, None, 'head'), may hold values from -0.109375 to 0.109375
- norm_gain: float32 [2, 128], replicated, may hold values from 1.2 to 2.2
- stale_kv: bfloat16 [16384, 2, 1536], P('patch', None, 'head'), may hold values from -4.5 to 4.5
- out_weight: bfloat16 [1536, 3072], P('head'), may hold values from -0.15625 to 0.15625
- stale_out: bfloat16 [16384, 3072], P('patch', 'head'), may hold values from -0.59765625 to 0.59765625
Outputs:
- layer_out: bfloat16 [16384, 3072], P('patch', 'head')
The draws below stay inside these ranges and needn't reach their ends.
Inputs may be any that keep to these rules, and one draw needn't show every extreme that they name: `refresh`: 1 marks a tile whose keys, values and output are recomputed; 0 one served by the previous step.
All inputs are finite; a program needn't handle non-finite values. No bound on the sum of `refresh` on one device may be relied on, other than what follows from the above.
Results may differ from the reference program's by a relative error of at most 0.015.
Values may be sent and summed in bfloat16 or wider, within the bound.
A program may use at most 128 MiB of HBM per device.

```python
import math
import jax
import jax.numpy as jnp
from jax import lax

D = 3072
HEADS = 12
HD = 128
TILE = 128
TILES = 128
TOKENS = 16384


def draw_stale_kv(key, part):
    key = jax.random.fold_in(key, 11)
    key_seed, sign_seed, size_seed, value_seed = jax.random.split(key, 4)
    row_width = HEADS * HD
    col_signs = (2 * jax.random.randint(sign_seed, (row_width,), 0, 2) - 1).astype(jnp.float32)
    key_rows = 1.5 * jax.random.truncated_normal(key_seed, -3.0, 3.0, (TOKENS, row_width), jnp.float32)
    offsets = col_signs * jax.random.uniform(size_seed, (row_width,), jnp.float32, 0.6, 1.4)
    value_noise = jax.random.truncated_normal(value_seed, -3.0, 3.0, (TOKENS, row_width), jnp.float32)
    value_rows = offsets[None, :] + value_noise
    return jnp.stack([key_rows, value_rows], axis=1).astype(jnp.bfloat16)


def set_ends(values, stream_key, least, top_value):
    shape = values.shape
    spot = [jax.random.randint(jax.random.fold_in(stream_key, axis), (), 0, shape[axis]) for axis in range(len(shape))]
    values = values.at[tuple(spot)].set(least)
    longest = shape.index(max(shape))
    spot[longest] = (spot[longest] + 1) % shape[longest]
    return values.at[tuple(spot)].set(top_value)


def steps_of(stream_key, shape, cuts, low, largest):
    gain = 1.0
    for position, shards_of in cuts:
        steps = jax.random.uniform(jax.random.fold_in(jax.random.fold_in(stream_key, 6), position), (shards_of,), jnp.float32, low / len(cuts), largest / len(cuts))
        gain = gain * jnp.repeat(jnp.exp(steps), shape[position] // shards_of).reshape((-1,) + (1,) * (len(shape) - 1 - position))
    return gain


def gaussian(rng, dims, spread, reach, shards=(), held_as=jnp.bfloat16):
    values = spread * jax.random.normal(rng, dims, jnp.float32)
    if shards:
        values = values * steps_of(rng, dims, shards, -0.22, 0.18)
    return jnp.clip(values, -reach, reach).astype(held_as)


def setup_inputs(seed: int = 0) -> dict:
    key_list = jax.random.split(jax.random.key(seed), 8)
    image_tokens = gaussian(key_list[0], (TOKENS, D), 1.0, 6.0, ((0, 64),))
    refresh = set_ends((jax.random.randint(key_list[1], (TILES,), 0, 2) < 1).astype(jnp.int32), jax.random.fold_in(key_list[1], 1), 0, 1)
    qkv_weight = gaussian(key_list[2], (D, 3, HEADS * HD), D ** -0.5, 0.109375, ((2, 4),))
    norm_gain = jnp.clip(jax.random.uniform(key_list[3], (2, HD), jnp.float32, 1.2, 2.2), 1.2, 2.2)
    stale_kv = draw_stale_kv(jax.random.fold_in(key_list[7], 71), 0)
    out_weight = gaussian(key_list[5], (HEADS * HD, D), (HEADS * HD) ** -0.5, 0.15625, ((0, 4),))
    stale_out = gaussian(key_list[6], (TOKENS, D), 0.1, 0.59765625, ((0, 64), (1, 4)))
    return {"image_tokens": image_tokens, "refresh": refresh, "qkv_weight": qkv_weight, "norm_gain": norm_gain, "stale_kv": stale_kv, "out_weight": out_weight, "stale_out": stale_out}


def rms_scale(values_in, gain_row):
    mean_square = lax.optimization_barrier(jnp.mean(values_in * values_in, axis=-1, keepdims=True))
    return values_in * lax.rsqrt(mean_square + 1e-06) * gain_row

def reference(image_tokens, refresh, qkv_weight, norm_gain, stale_kv, out_weight, stale_out):
    fresh_proj = jnp.dot(image_tokens, qkv_weight.reshape(D, 3 * HEADS * HD), preferred_element_type=jnp.float32)
    fresh_proj = fresh_proj.reshape(TOKENS, 3, HEADS, HD)
    queries = rms_scale(fresh_proj[:, 0], norm_gain[0]).astype(jnp.bfloat16)
    key_new = rms_scale(fresh_proj[:, 1], norm_gain[1]).astype(jnp.bfloat16)
    value_new = fresh_proj[:, 2].astype(jnp.bfloat16)
    marked = jnp.repeat(refresh, TILE) > 0
    keys_now = jnp.where(marked[:, None, None], key_new, stale_kv[:, 0].reshape(TOKENS, HEADS, HD))
    values_now = jnp.where(marked[:, None, None], value_new, stale_kv[:, 1].reshape(TOKENS, HEADS, HD))
    keys_wide = keys_now.astype(jnp.float32)
    values_wide = values_now.astype(jnp.float32)
    score_scale = 1.0 / math.sqrt(HD)
    query_blocks = queries.reshape(TOKENS // TILE, TILE, HEADS, HD)

    def attend(query_block):
        scores = jnp.einsum('qhd,khd->hqk', query_block.astype(jnp.float32), keys_wide) * score_scale
        weights = jnp.exp(scores)
        denominator = lax.optimization_barrier(jnp.sum(weights, axis=-1))
        rounded = lax.optimization_barrier(weights.astype(jnp.bfloat16)).astype(jnp.float32)
        numerator = jnp.einsum('hqk,khd->qhd', rounded, values_wide)
        return (numerator / jnp.transpose(denominator)[:, :, None]).astype(jnp.bfloat16)
    attended = lax.map(attend, query_blocks).reshape(TOKENS, HEADS * HD)
    projected = jnp.dot(attended, out_weight, preferred_element_type=jnp.float32).astype(jnp.bfloat16)
    return jnp.where(marked[:, None], projected, stale_out)
```

```python
import functools
import math

import jax
import jax.numpy as jnp
from jax import lax
from jax.experimental import pallas as pl
from jax.experimental.pallas import tpu as pltpu
from jax.sharding import Mesh
from jax.sharding import PartitionSpec as P

SPLIT = ("x", "yh", "z", "yl", "core")


def rms_scale(values_in, gain_row):
    mean_square = jnp.mean(values_in * values_in, axis=-1, keepdims=True)
    return values_in * lax.rsqrt(mean_square + 1e-06) * gain_row


def attend_kernel(q_ref, kv_ref, num_ref, den_ref, acc_ref):
    step = pl.program_id(1)

    @pl.when(step == 0)
    def _():
        acc_ref[...] = jnp.zeros_like(acc_ref)

    rows = q_ref.shape[1]
    keys = kv_ref.shape[2]
    key_block = kv_ref[0, 0]
    value_block = jnp.concatenate(
        [kv_ref[0, 1], jnp.ones((keys, 128), jnp.bfloat16)], axis=1
    )

    def body(i, carry):
        span = pl.ds(pl.multiple_of(i * 256, 256), 256)
        scores = lax.dot_general(
            q_ref[0, span], key_block, (((1,), (1,)), ((), ())),
            preferred_element_type=jnp.float32,
        )
        weights = jnp.exp2(scores).astype(jnp.bfloat16)
        acc_ref[span] += jnp.dot(weights, value_block, preferred_element_type=jnp.float32)
        return carry

    lax.fori_loop(0, rows // 256, body, 0)

    @pl.when(step == pl.num_programs(1) - 1)
    def _():
        num_ref[0] = acc_ref[:, :128]
        den_ref[0] = acc_ref[:, 128:]


def attend(q, kv):
    heads, rows, width = q.shape
    keys = kv.shape[2]
    block = 1024
    return pl.pallas_call(
        attend_kernel,
        grid=(heads, keys // block),
        in_specs=[
            pl.BlockSpec((1, rows, width), lambda h, s: (h, 0, 0)),
            pl.BlockSpec((1, 2, block, width), lambda h, s: (h, 0, s, 0)),
        ],
        out_specs=[
            pl.BlockSpec((1, rows, width), lambda h, s: (h, 0, 0)),
            pl.BlockSpec((1, rows, width), lambda h, s: (h, 0, 0)),
        ],
        out_shape=[
            jax.ShapeDtypeStruct((heads, rows, width), jnp.float32),
            jax.ShapeDtypeStruct((heads, rows, width), jnp.float32),
        ],
        scratch_shapes=[pltpu.VMEM((rows, 2 * width), jnp.float32)],
    )(q, kv)


def swap(array):
    pairs = []
    for t in range(2):
        for low in range(2):
            for g in range(2):
                pairs.append((t * 4 + low * 2 + g, g * 4 + (1 - low) * 2 + t))
    return lax.ppermute(array, ("yh", "yl", "core"), pairs)


def local(image_tokens, refresh, qkv_weight, norm_gain, stale_kv, out_weight, stale_out):
    rows, model_width = image_tokens.shape
    group_width = qkv_weight.shape[2]
    width = norm_gain.shape[1]
    heads = group_width // width
    tile_rows = rows // refresh.shape[0]
    scale = math.log2(math.e) / math.sqrt(width)
    weight = jnp.transpose(qkv_weight, (1, 0, 2))
    marked = jnp.repeat(refresh, tile_rows) > 0
    fresh = [
        jnp.dot(image_tokens, weight[j], preferred_element_type=jnp.float32).reshape(rows, heads, width)
        for j in range(3)
    ]
    queries = rms_scale(fresh[0], norm_gain[0] * scale).astype(jnp.bfloat16)
    key_new = rms_scale(fresh[1], norm_gain[1]).astype(jnp.bfloat16)
    value_new = fresh[2].astype(jnp.bfloat16)
    stale = stale_kv.reshape(rows, 2, heads, width)
    pick = marked[:, None, None]
    current = jnp.stack(
        [queries, jnp.where(pick, key_new, stale[:, 0]), jnp.where(pick, value_new, stale[:, 1])]
    )
    current = swap(jnp.transpose(current, (2, 0, 1, 3)))
    q = lax.all_gather(current[:, 0], "x", axis=1, tiled=True)
    kv = lax.all_gather(current[:, 1:], ("z", "core"), axis=2, tiled=True)
    numerator, denominator = attend(q, kv)
    numerator = lax.psum_scatter(numerator.astype(jnp.bfloat16), "x", scatter_dimension=1, tiled=True)
    denominator = lax.psum_scatter(denominator[:, :, 0], "x", scatter_dimension=1, tiled=True)
    attended = (numerator.astype(jnp.float32) / denominator[:, :, None]).astype(jnp.bfloat16)
    attended = jnp.transpose(swap(attended), (1, 0, 2)).reshape(rows, group_width)
    projected = jnp.dot(attended, out_weight, preferred_element_type=jnp.float32)
    own_columns = lax.psum_scatter(
        projected.astype(jnp.bfloat16), ("yl", "core"), scatter_dimension=1, tiled=True
    )
    return jnp.where(marked[:, None], own_columns, stale_out)


def solution(mesh):
    split = Mesh(mesh.devices.reshape(4, 2, 8, 2, 2), SPLIT)
    patch, head = ("x", "yh", "z"), ("yl", "core")
    placed = (
        P(patch, None),
        P(patch),
        P(None, None, head),
        P(),
        P(patch, None, head),
        P(head, None),
        P(patch, head),
    )
    return jax.shard_map(
        local, mesh=split, in_specs=placed, out_specs=P(patch, head), check_vma=False
    )
```

```python
import functools
import math

import jax
import jax.numpy as jnp
from jax import lax
from jax.experimental import pallas as pl
from jax.experimental.pallas import tpu as pltpu
from jax.sharding import PartitionSpec as P

MESH = pl.DeviceIdType.MESH
ROWS_BY_ROWS = (((1,), (1,)), ((), ()))
COLUMNS_BY_COLUMNS = (((0,), (0,)), ((), ()))


def kernel(
    nx, nz,
    tokens, refresh, qkv_weight, gain, stale_kv, out_weight, stale_out,
    out,
    weight_buf, stage, kv_buf, q_buf, acc, den,
    num_stage, num_in, den_in, att_stage, att_all, out_weight_all,
    load_sem, own_sem,
    swap_s, swap_r, x_s, x_r, z_s, z_r, sib_s, sib_r, w_s, w_r, sum_s, sum_r, att_s, att_r,
):
    heads, _, rows, width = stage.shape
    half = nz // 2
    out_cols = stale_out.shape[1]
    tile_rows = rows // refresh.shape[0]
    patch, head = lax.axis_index("patch"), lax.axis_index("head")
    x, yh, z = patch // (2 * nz), (patch // nz) % 2, patch % nz
    yl, core = head // 2, head % 2

    def device(x_to, yh_to, z_to, yl_to, core_to):
        return ((x_to * 2 + yh_to) * nz + z_to, yl_to * 2 + core_to)

    sibling = device(x, yh, z, yl, 1 - core)
    swapped = device(x, core, z, 1 - yl, yh)
    along_z = (
        device(x, yh, (z + 1) % nz, yl, core),
        device(x, yh, (z + nz - 1) % nz, yl, core),
    )

    def along_x(step):
        return device((x + step) % nx, yh, z, yl, core)

    def send(src, dst, send_sem, recv_sem, to):
        return pltpu.make_async_remote_copy(
            src_ref=src, dst_ref=dst, send_sem=send_sem, recv_sem=recv_sem,
            device_id=to, device_id_type=MESH,
        )

    def load(h, j):
        return pltpu.make_async_copy(
            qkv_weight.at[j, :, pl.ds(pl.multiple_of(h * width, width), width)],
            weight_buf.at[h, :, pl.ds(j * width, width)],
            load_sem.at[h, j],
        )

    def swap_kv(h):
        return send(stage.at[h, pl.ds(1, 2)], kv_buf.at[h, :, 0], swap_s.at[h, 0], swap_r.at[h, 0], swapped)

    def swap_q(h):
        return send(stage.at[h, 0], q_buf.at[h, 0], swap_s.at[h, 1], swap_r.at[h, 1], swapped)

    def gather_x(h, j):
        return send(q_buf.at[h, 0], q_buf.at[h, j], x_s.at[h, j - 1], x_r.at[h, j - 1], along_x(j))

    def spot(s, way):
        return 0 if s == 0 else 4 * s - 2 + way

    def ring(h, s, way):
        if s < half - 1:
            src, dst = kv_buf.at[h, :, spot(s, way)], kv_buf.at[h, :, spot(s + 1, way)]
        else:
            src, dst = kv_buf.at[h, way, spot(s, way)], kv_buf.at[h, way, 4 * half - 2]
        return send(src, dst, z_s.at[h, s, way], z_r.at[h, s, way], along_z[way])

    def share(h, s, first, count):
        return send(
            kv_buf.at[h, :, pl.ds(first, count)], kv_buf.at[h, :, pl.ds(first + count, count)],
            sib_s.at[h, s], sib_r.at[h, s], sibling,
        )

    def share_own(h):
        return share(h, 0, 0, 1)

    def share_step(h, s):
        return share(h, s, 4 * s - 2, 2)

    def share_last(h):
        return share(h, half, 4 * half - 2, 1)

    group = yl * 2 + core
    cross_yh = (yh + core) % 2

    def weight_columns(block):
        return out_weight.at[:, :, pl.ds(pl.multiple_of(block * out_cols, out_cols), out_cols)]

    def weight_own():
        return pltpu.make_async_copy(weight_columns(group), out_weight_all.at[:, group], own_sem)

    def weight_sibling(slot):
        return send(
            weight_columns(yl * 2 + 1 - core), out_weight_all.at[:, slot],
            w_s.at[2], w_r.at[2], sibling,
        )

    def weight_cross(c, slot, source_core):
        return send(
            weight_columns((1 - yl) * 2 + c), out_weight_all.at[:, slot],
            w_s.at[c], w_r.at[source_core], device(x, cross_yh, z, 1 - yl, c),
        )

    def sum_num(h, j):
        return send(
            num_stage.at[h, j - 1], num_in.at[h, j - 1],
            sum_s.at[h, j - 1, 0], sum_r.at[h, j - 1, 0], along_x(nx - j),
        )

    def sum_den(h, j):
        return send(
            den.at[h, :, pl.ds(j * rows, rows)], den_in.at[h, j - 1],
            sum_s.at[h, j - 1, 1], sum_r.at[h, j - 1, 1], along_x(nx - j),
        )

    held_group = (1 - yl) * 2 + yh

    def hand_out(h, d, slot):
        return send(
            att_stage.at[h], att_all.at[h, slot],
            att_s.at[h, d], att_r.at[h, slot], device(x, core, z, d // 2, d % 2),
        )

    def compute(h, first, count, fresh):
        keys = kv_buf[h, 0, pl.ds(first, count)].reshape(count * rows, width)
        values = kv_buf[h, 1, pl.ds(first, count)].reshape(count * rows, width)
        scores = lax.dot_general(
            keys, q_buf[h].reshape(nx * rows, width), ROWS_BY_ROWS, preferred_element_type=jnp.float32
        )
        weights = jnp.exp2(scores)
        part = jnp.sum(weights.reshape(count * rows // 8, 8, nx * rows), axis=0)
        product = lax.dot_general(
            values, weights.astype(jnp.bfloat16), COLUMNS_BY_COLUMNS, preferred_element_type=jnp.float32
        )
        if fresh:
            acc[h], den[h] = product, part
        else:
            acc[h] += product
            den[h] += part

    def marked(i, shape):
        return jnp.broadcast_to(refresh[i], shape) > 0

    def normed(part, row):
        mean_square = jnp.mean(part * part, axis=-1, keepdims=True)
        return part * lax.rsqrt(mean_square + 1e-06) * row

    for h in range(heads):
        for j in range(3):
            load(h, j).start()

    barrier = pltpu.get_barrier_semaphore()
    peers = [along_x(j) for j in range(1, nx)] + list(along_z)
    for other in range(1, 8):
        bits = (other // 4, (other // 2) % 2, other % 2)
        peers.append(device(x, (yh + bits[0]) % 2, z, (yl + bits[1]) % 2, (core + bits[2]) % 2))
    for peer in peers:
        pl.semaphore_signal(barrier, inc=1, device_id=peer, device_id_type=MESH)
    pl.semaphore_wait(barrier, len(peers))

    scale = math.log2(math.e) / math.sqrt(width)
    query_gain = gain[pl.ds(0, 1), :] * scale
    key_gain = gain[pl.ds(1, 1), :]

    def project(h, carry):
        for j in range(3):
            load(h, j).wait()
        fresh = jnp.dot(tokens[...], weight_buf[h], preferred_element_type=jnp.float32)
        stage[h, 0] = normed(fresh[:, :width], query_gain).astype(jnp.bfloat16)
        current = (normed(fresh[:, width : 2 * width], key_gain), fresh[:, 2 * width :])
        for j in range(2):
            for i in range(refresh.shape[0]):
                span = slice(i * tile_rows, (i + 1) * tile_rows)
                stale = stale_kv[h, j, span].astype(jnp.float32)
                stage[h, 1 + j, span] = jnp.where(
                    marked(i, stale.shape), current[j][span], stale
                ).astype(jnp.bfloat16)
        swap_kv(h).start()
        swap_q(h).start()
        return carry

    lax.fori_loop(0, heads, project, 0)

    def distribute(h, carry):
        swap_kv(h).wait_recv()
        for way in range(2):
            ring(h, 0, way).start()
        share_own(h).start()
        swap_q(h).wait_recv()
        for j in range(1, nx):
            gather_x(h, j).start()
        return carry

    lax.fori_loop(0, heads, distribute, 0)
    weight_own().start()
    weight_sibling(group).start()
    for c in range(2):
        weight_cross(c, group, core).start()

    for s in range(1, half):

        def event(h, carry, s=s):
            for way in range(2):
                ring(h, s - 1, way).wait_recv()
            for way in range(2):
                ring(h, s, way).start()
            share_step(h, s).start()
            if s == 1:
                for j in range(1, nx):
                    gather_x(h, j).wait_recv()
                share_own(h).wait_recv()
                compute(h, 0, 2, True)

                @pl.when(h > 0)
                def _():
                    share_step(h - 1, 1).wait_recv()
                    compute(h - 1, 2, 4, False)
            else:
                late_h = (h + heads - 1) % heads
                late_s = s - jnp.where(h == 0, 1, 0)
                share_step(late_h, late_s).wait_recv()
                compute(late_h, 4 * late_s - 2, 4, False)
            return carry

        lax.fori_loop(0, heads, event, 0)

    share_step(heads - 1, half - 1).wait_recv()
    compute(heads - 1, 4 * half - 6, 4, False)

    def finish(h):
        share_last(h).wait_recv()
        compute(h, 4 * half - 2, 2, False)
        for j in range(1, nx):
            num_stage[h, j - 1] = acc[h, :, j * rows : (j + 1) * rows].astype(jnp.bfloat16)
            sum_num(h, j).start()
            sum_den(h, j).start()

    def last_event(h, carry):
        for way in range(2):
            ring(h, half - 1, way).wait_recv()
        share_last(h).start()

        @pl.when(h > 0)
        def _():
            finish(h - 1)

        return carry

    lax.fori_loop(0, heads, last_event, 0)
    finish(heads - 1)

    def attended(h, carry):
        numerator = acc[h, :, :rows]
        denominator = den[h, :, :rows]
        for j in range(1, nx):
            sum_num(h, j).wait_recv()
            sum_den(h, j).wait_recv()
            numerator += num_in[h, j - 1].astype(jnp.float32)
            denominator += den_in[h, j - 1]
        denominator = jnp.sum(denominator, axis=0, keepdims=True)
        result = (numerator / denominator).astype(jnp.bfloat16)
        att_stage[h] = result
        for d in range(4):

            @pl.when(jnp.logical_or(yh != core, head != d))
            def _(d=d):
                hand_out(h, d, held_group).start()

        @pl.when(yh == core)
        def _():
            att_all[h, held_group] = result

        return carry

    lax.fori_loop(0, heads, attended, 0)

    weight_own().wait()
    weight_sibling(yl * 2 + 1 - core).wait_recv()
    for source_core in range(2):
        weight_cross(0, (1 - yl) * 2 + source_core, source_core).wait_recv()
    total = None
    for h in range(heads):
        for slot in range(4):

            @pl.when(jnp.logical_or(yh != core, held_group != slot))
            def _(h=h, slot=slot):
                hand_out(h, 0, slot).wait_recv()

        part = lax.dot_general(
            att_all[h].reshape(4 * width, rows),
            out_weight_all[h].reshape(4 * width, out_cols),
            COLUMNS_BY_COLUMNS,
            preferred_element_type=jnp.float32,
        )
        total = part if total is None else total + part
    for i in range(refresh.shape[0]):
        span = slice(i * tile_rows, (i + 1) * tile_rows)
        stale = stale_out[span].astype(jnp.float32)
        out[span] = jnp.where(marked(i, stale.shape), total[span], stale).astype(jnp.bfloat16)

    weight_sibling(group).wait_send()
    for c in range(2):
        weight_cross(c, group, core).wait_send()

    def drain(h, carry):
        swap_kv(h).wait_send()
        swap_q(h).wait_send()
        for j in range(1, nx):
            gather_x(h, j).wait_send()
            sum_num(h, j).wait_send()
            sum_den(h, j).wait_send()
        for s in range(half):
            for way in range(2):
                ring(h, s, way).wait_send()
        share_own(h).wait_send()
        for s in range(1, half):
            share_step(h, s).wait_send()
        share_last(h).wait_send()
        for d in range(4):

            @pl.when(jnp.logical_or(yh != core, head != d))
            def _(d=d):
                hand_out(h, d, held_group).wait_send()

        return carry

    lax.fori_loop(0, heads, drain, 0)


def local(nx, nz, image_tokens, refresh, qkv_weight, norm_gain, stale_kv, out_weight, stale_out):
    rows, model_width = image_tokens.shape
    group_width = qkv_weight.shape[2]
    width = norm_gain.shape[1]
    heads = group_width // width
    half = nz // 2
    out_cols = stale_out.shape[1]
    weight = jnp.transpose(qkv_weight, (1, 0, 2))
    stale = jnp.transpose(stale_kv.reshape(rows, 2, heads, width), (2, 1, 0, 3))
    bf16, f32 = jnp.bfloat16, jnp.float32
    dma = pltpu.SemaphoreType.DMA
    vmem = pl.BlockSpec(memory_space=pltpu.VMEM)
    smem = pl.BlockSpec(memory_space=pltpu.SMEM)
    anywhere = pl.BlockSpec(memory_space=pl.ANY)
    return pl.pallas_call(
        functools.partial(kernel, nx, nz),
        out_shape=jax.ShapeDtypeStruct((rows, out_cols), bf16),
        in_specs=[vmem, smem, anywhere, vmem, vmem, anywhere, vmem],
        out_specs=vmem,
        scratch_shapes=[
            pltpu.VMEM((heads, model_width, 3 * width), bf16),
            pltpu.VMEM((heads, 3, rows, width), bf16),
            pltpu.VMEM((heads, 2, 4 * half, rows, width), bf16),
            pltpu.VMEM((heads, nx, rows, width), bf16),
            pltpu.VMEM((heads, width, nx * rows), f32),
            pltpu.VMEM((heads, 8, nx * rows), f32),
            pltpu.VMEM((heads, nx - 1, width, rows), bf16),
            pltpu.VMEM((heads, nx - 1, width, rows), bf16),
            pltpu.VMEM((heads, nx - 1, 8, rows), f32),
            pltpu.VMEM((heads, width, rows), bf16),
            pltpu.VMEM((heads, 4, width, rows), bf16),
            pltpu.VMEM((heads, 4, width, out_cols), bf16),
            dma((heads, 3)), dma,
            dma((heads, 2)), dma((heads, 2)),
            dma((heads, nx - 1)), dma((heads, nx - 1)),
            dma((heads, half, 2)), dma((heads, half, 2)),
            dma((heads, half + 1)), dma((heads, half + 1)),
            dma((3,)), dma((3,)),
            dma((heads, nx - 1, 2)), dma((heads, nx - 1, 2)),
            dma((heads, 4)), dma((heads, 4)),
        ],
        compiler_params=pltpu.CompilerParams(
            collective_id=0, has_side_effects=True, vmem_limit_bytes=50 << 20
        ),
    )(
        image_tokens, refresh, weight, norm_gain, stale,
        out_weight.reshape(heads, width, out_weight.shape[1]), stale_out,
    )


def solution(mesh, nx=4, nz=8):
    placed = (
        P("patch", None),
        P("patch"),
        P(None, None, "head"),
        P(),
        P("patch", None, "head"),
        P("head", None),
        P("patch", "head"),
    )
    return jax.shard_map(
        functools.partial(local, nx, nz),
        mesh=mesh, in_specs=placed, out_specs=P("patch", "head"), check_vma=False,
    )
```

```python
import functools
import math

import jax
import jax.numpy as jnp
from jax import lax
from jax.experimental import pallas as pl
from jax.experimental.pallas import tpu as pltpu
from jax.sharding import PartitionSpec as P

MESH = pl.DeviceIdType.MESH
ROWS_BY_ROWS = (((1,), (1,)), ((), ()))
COLUMNS_BY_COLUMNS = (((0,), (0,)), ((), ()))


def kernel(
    nx, nz,
    tokens_far, refresh_far, qkv_weight, gain_far, stale_kv_far, out_weight, stale_out_far,
    out,
    tokens, refresh, gain, stale_kv, stale_out,
    kv_weight, q_weight, stage, kv_buf, q_buf, acc, den,
    num_stage, num_in, den_in, att_stage, att_all, out_weight_all,
    load_sem, own_sem,
    swap_s, swap_r, x_s, x_r, z_s, z_r, sib_s, sib_r, w_s, w_r, sum_s, sum_r, att_s, att_r,
):
    heads, _, rows, width = stage.shape
    half = nz // 2
    out_cols = stale_out.shape[1]
    tiles = refresh.shape[0]
    tile_rows = rows // tiles
    patch, head = lax.axis_index("patch"), lax.axis_index("head")
    x, yh, z = patch // (2 * nz), (patch // nz) % 2, patch % nz
    yl, core = head // 2, head % 2

    def device(x_to, yh_to, z_to, yl_to, core_to):
        return ((x_to * 2 + yh_to) * nz + z_to, yl_to * 2 + core_to)

    sibling = device(x, yh, z, yl, 1 - core)
    swapped = device(x, core, z, 1 - yl, yh)
    along_z = (
        device(x, yh, (z + 1) % nz, yl, core),
        device(x, yh, (z + nz - 1) % nz, yl, core),
    )

    def along_x(step):
        return device((x + step) % nx, yh, z, yl, core)

    def send(src, dst, send_sem, recv_sem, to):
        return pltpu.make_async_remote_copy(
            src_ref=src, dst_ref=dst, send_sem=send_sem, recv_sem=recv_sem,
            device_id=to, device_id_type=MESH,
        )

    def load_kv_weight(h, j):
        return pltpu.make_async_copy(
            qkv_weight.at[1 + j, :, pl.ds(h * width, width)],
            kv_weight.at[h, :, pl.ds(j * width, width)],
            load_sem.at[2 * h + j],
        )

    def load(far, near, index):
        return pltpu.make_async_copy(far, near, load_sem.at[2 * heads + index])

    load_tokens = load(tokens_far, tokens, 0)
    load_refresh = load(refresh_far, refresh, 1)
    load_gain = load(gain_far, gain, 2)
    load_stale_kv = load(stale_kv_far, stale_kv, 3)
    load_stale_out = load(stale_out_far, stale_out, 4)
    load_q_weight = load(qkv_weight.at[0], q_weight, 5)

    def swap(h, j):
        dst = q_buf.at[h, 0] if j == 0 else kv_buf.at[h, j - 1, 0]
        return send(stage.at[h, j], dst, swap_s.at[h, j], swap_r.at[h, j], swapped)

    def gather_x(h, j):
        return send(q_buf.at[h, 0], q_buf.at[h, j], x_s.at[h, j - 1], x_r.at[h, j - 1], along_x(j))

    def spot(s, way):
        return 4 * s - 2 + way

    def move(h, s, way, c, src, dst):
        return send(src, dst, z_s.at[h, s, way, c], z_r.at[h, s, way, c], along_z[way])

    def ring_own(h, way, c):
        return move(h, 0, way, c, kv_buf.at[h, c, 0], kv_buf.at[h, c, spot(1, way)])

    def ring(h, s, way, c):
        return move(h, s, way, c, kv_buf.at[h, c, spot(s, way)], kv_buf.at[h, c, spot(s + 1, way)])

    def ring_last(h, way):
        s = half - 1
        return move(h, s, way, way, kv_buf.at[h, way, spot(s, way)], kv_buf.at[h, way, 4 * half - 2])

    def landed(h, s, way, c):
        here = kv_buf.at[h, c, spot(s, way)]
        return move(h, s - 1, way, c, here, here)

    def share(h, s, first, count):
        return send(
            kv_buf.at[h, :, pl.ds(first, count)], kv_buf.at[h, :, pl.ds(first + count, count)],
            sib_s.at[h, s], sib_r.at[h, s], sibling,
        )

    def share_own(h):
        return share(h, 0, 0, 1)

    def share_step(h, s):
        return share(h, s, 4 * s - 2, 2)

    def share_last(h):
        return share(h, half, 4 * half - 2, 1)

    group = yl * 2 + core
    cross_yh = (yh + core) % 2

    def weight_columns(block):
        return out_weight.at[:, :, pl.ds(pl.multiple_of(block * out_cols, out_cols), out_cols)]

    def weight_own():
        return pltpu.make_async_copy(weight_columns(group), out_weight_all.at[:, group], own_sem)

    def weight_sibling(slot):
        return send(
            weight_columns(yl * 2 + 1 - core), out_weight_all.at[:, slot],
            w_s.at[2], w_r.at[2], sibling,
        )

    def weight_cross(c, slot, source_core):
        return send(
            weight_columns((1 - yl) * 2 + c), out_weight_all.at[:, slot],
            w_s.at[c], w_r.at[source_core], device(x, cross_yh, z, 1 - yl, c),
        )

    def sum_num(h, j, i):
        return send(
            num_stage.at[h, j - 1, i], num_in.at[h, j - 1, i],
            sum_s.at[h, j - 1, i], sum_r.at[h, j - 1, i], along_x(nx - j),
        )

    def sum_den(h, j):
        return send(
            den.at[h, :, pl.ds(j * rows, rows)], den_in.at[h, j - 1],
            sum_s.at[h, j - 1, tiles], sum_r.at[h, j - 1, tiles], along_x(nx - j),
        )

    held_group = (1 - yl) * 2 + yh

    def hand_out(h, i, d, slot):
        return send(
            att_stage.at[h, i], att_all.at[h, i, slot],
            att_s.at[h, i, d], att_r.at[h, i, slot], device(x, core, z, d // 2, d % 2),
        )

    def compute(h, first, count, fresh):
        keys = kv_buf[h, 0, pl.ds(first, count)].reshape(count * rows, width)
        values = kv_buf[h, 1, pl.ds(first, count)].reshape(count * rows, width)
        scores = lax.dot_general(
            keys, q_buf[h].reshape(nx * rows, width), ROWS_BY_ROWS, preferred_element_type=jnp.float32
        )
        weights = jnp.exp2(scores)
        part = jnp.sum(weights.reshape(count * rows // 8, 8, nx * rows), axis=0)
        product = lax.dot_general(
            values, weights.astype(jnp.bfloat16), COLUMNS_BY_COLUMNS, preferred_element_type=jnp.float32
        )
        if fresh:
            acc[h], den[h] = product, part
        else:
            acc[h] += product
            den[h] += part

    def marked(i, shape):
        return jnp.broadcast_to(refresh[i], shape) > 0

    def normed(part, row):
        mean_square = jnp.mean(part * part, axis=-1, keepdims=True)
        return part * lax.rsqrt(mean_square + 1e-06) * row

    load_tokens.start()
    for j in range(2):
        load_kv_weight(0, j).start()
        if j == 0:
            for copy in (load_gain, load_refresh, load_stale_kv):
                copy.start()

    barrier = pltpu.get_barrier_semaphore()
    peers = [along_x(j) for j in range(1, nx)] + list(along_z)
    for other in range(1, 8):
        bits = (other // 4, (other // 2) % 2, other % 2)
        peers.append(device(x, (yh + bits[0]) % 2, z, (yl + bits[1]) % 2, (core + bits[2]) % 2))
    for peer in peers:
        pl.semaphore_signal(barrier, inc=1, device_id=peer, device_id_type=MESH)

    load_tokens.wait()
    load_kv_weight(0, 0).wait()
    for h in range(1, heads):
        for j in range(2):
            load_kv_weight(h, j).start()
    load_q_weight.start()
    load_stale_out.start()
    for copy in (load_gain, load_refresh, load_stale_kv):
        copy.wait()
    scale = math.log2(math.e) / math.sqrt(width)
    query_gain = gain[pl.ds(0, 1), :] * scale
    key_gain = gain[pl.ds(1, 1), :]

    def place(h, j, fresh):
        stale = stale_kv[:, :, h * width : (h + 1) * width].astype(jnp.float32)
        for i in range(tiles):
            span = slice(i * tile_rows, (i + 1) * tile_rows)
            kept = stale[span, j, :]
            stage[h, 1 + j, span] = jnp.where(marked(i, kept.shape), fresh[span], kept).astype(jnp.bfloat16)
        if h == 0 and j == 0:
            pl.semaphore_wait(barrier, len(peers))
        swap(h, 1 + j).start()

    def project(h, columns):
        return jnp.dot(tokens[...], kv_weight[h, :, columns], preferred_element_type=jnp.float32)

    place(0, 0, normed(project(0, slice(0, width)), key_gain))
    load_kv_weight(0, 1).wait()
    place(0, 1, project(0, slice(width, 2 * width)))
    for h in range(1, heads):
        for j in range(2):
            load_kv_weight(h, j).wait()
        fresh = project(h, slice(0, 2 * width))
        place(h, 0, normed(fresh[:, :width], key_gain))
        place(h, 1, fresh[:, width:])

    load_q_weight.wait()
    fresh = jnp.dot(tokens[...], q_weight[...], preferred_element_type=jnp.float32)
    for h in range(heads):
        stage[h, 0] = normed(fresh[:, h * width : (h + 1) * width], query_gain).astype(jnp.bfloat16)
        swap(h, 0).start()

    def distribute_kv(h, carry):
        for c in range(2):
            swap(h, 1 + c).wait_recv()
            for way in range(2):
                ring_own(h, way, c).start()
        share_own(h).start()
        return carry

    def distribute_q(h, carry):
        swap(h, 0).wait_recv()
        for j in range(1, nx):
            gather_x(h, j).start()
        return carry

    lax.fori_loop(0, heads, distribute_kv, 0)
    lax.fori_loop(0, heads, distribute_q, 0)
    weight_own().start()
    weight_sibling(group).start()
    for c in range(2):
        weight_cross(c, group, core).start()

    order = sorted(
        ((h, s) for h in range(heads) for s in range(1, half + 1)),
        key=lambda pair: (pair[0] + 2 * pair[1], pair[0]),
    )

    def look_up(i):
        h, s = order[0]
        for place, (h_there, s_there) in enumerate(order):
            h = jnp.where(i == place, h_there, h)
            s = jnp.where(i == place, s_there, s)
        return h, s

    def arrive(h, s):
        @pl.when(s < half - 1)
        def _():
            for turned in range(2):
                for way in range(2):
                    c = (way + turned) % 2
                    landed(h, s, way, c).wait_recv()
                    ring(h, s, way, c).start()

        @pl.when(s == half - 1)
        def _():
            for way in range(2):
                landed(h, s, way, way).wait_recv()
                ring_last(h, way).start()
            for way in range(2):
                landed(h, s, way, 1 - way).wait_recv()

        @pl.when(s < half)
        def _():
            share_step(h, s).start()

        @pl.when(s == half)
        def _():
            for way in range(2):
                ring_last(h, way).wait_recv()
            share_last(h).start()

    def work(h, s):
        @pl.when(s == 1)
        def _():
            for j in range(1, nx):
                gather_x(h, j).wait_recv()
            share_own(h).wait_recv()
            compute(h, 0, 2, True)

        @pl.when(s < half)
        def _():
            share_step(h, s).wait_recv()
            compute(h, 4 * s - 2, 4, False)

        @pl.when(s == half)
        def _():
            share_last(h).wait_recv()
            compute(h, 4 * half - 2, 2, False)
            for j in range(1, nx):
                sum_den(h, j).start()
            for i in range(tiles):
                for j in range(1, nx):
                    first = j * rows + i * tile_rows
                    num_stage[h, j - 1, i] = acc[h, :, first : first + tile_rows].astype(jnp.bfloat16)
                    sum_num(h, j, i).start()

    def turn(i, carry):
        @pl.when(i < len(order))
        def _():
            arrive(*look_up(i))

        @pl.when(i > 0)
        def _():
            work(*look_up(i - 1))

        return carry

    lax.fori_loop(0, len(order) + 1, turn, 0)

    def drain_early(h, carry):
        for j in range(3):
            swap(h, j).wait_send()
        for j in range(1, nx):
            gather_x(h, j).wait_send()
        for way in range(2):
            for c in range(2):
                ring_own(h, way, c).wait_send()
                for s in range(1, half - 1):
                    ring(h, s, way, c).wait_send()
            ring_last(h, way).wait_send()
        share_own(h).wait_send()
        for s in range(1, half):
            share_step(h, s).wait_send()
        share_last(h).wait_send()
        return carry

    lax.fori_loop(0, heads, drain_early, 0)
    weight_own().wait()
    weight_sibling(yl * 2 + 1 - core).wait_recv()
    weight_sibling(group).wait_send()
    for c in range(2):
        weight_cross(c, (1 - yl) * 2 + c, c).wait_recv()
        weight_cross(c, group, core).wait_send()
    load_stale_out.wait()

    def attended(h, carry):
        denominator = den[h, :, :rows]
        for j in range(1, nx):
            sum_den(h, j).wait_recv()
            denominator += den_in[h, j - 1]
        denominator = jnp.sum(denominator, axis=0, keepdims=True)
        for i in range(tiles):
            span = slice(i * tile_rows, (i + 1) * tile_rows)
            numerator = acc[h, :, span]
            for j in range(1, nx):
                sum_num(h, j, i).wait_recv()
                numerator += num_in[h, j - 1, i].astype(jnp.float32)
            result = (numerator / denominator[:, span]).astype(jnp.bfloat16)
            att_stage[h, i] = result
            for d in range(4):

                @pl.when(jnp.logical_or(yh != core, head != d))
                def _(d=d, i=i):
                    hand_out(h, i, d, held_group).start()

            @pl.when(yh == core)
            def _(i=i, result=result):
                att_all[h, i, held_group] = result

        return carry

    lax.fori_loop(0, heads, attended, 0)

    def drain_sums(h, carry):
        for j in range(1, nx):
            sum_den(h, j).wait_send()
            for i in range(tiles):
                sum_num(h, j, i).wait_send()
        return carry

    lax.fori_loop(0, heads, drain_sums, 0)

    total = [None] * tiles
    for h in range(heads):
        for i in range(tiles):
            for slot in range(4):

                @pl.when(jnp.logical_or(yh != core, held_group != slot))
                def _(h=h, i=i, slot=slot):
                    hand_out(h, i, 0, slot).wait_recv()

            part = lax.dot_general(
                att_all[h, i].reshape(4 * width, tile_rows),
                out_weight_all[h].reshape(4 * width, out_cols),
                COLUMNS_BY_COLUMNS,
                preferred_element_type=jnp.float32,
            )
            total[i] = part if h == 0 else total[i] + part
            if h == heads - 1:
                span = slice(i * tile_rows, (i + 1) * tile_rows)
                stale = stale_out[span].astype(jnp.float32)
                out[span] = jnp.where(marked(i, stale.shape), total[i], stale).astype(jnp.bfloat16)

    def drain_late(h, carry):
        for i in range(tiles):
            for d in range(4):

                @pl.when(jnp.logical_or(yh != core, head != d))
                def _(i=i, d=d):
                    hand_out(h, i, d, held_group).wait_send()

        return carry

    lax.fori_loop(0, heads, drain_late, 0)


def local(nx, nz, image_tokens, refresh, qkv_weight, norm_gain, stale_kv, out_weight, stale_out):
    rows, model_width = image_tokens.shape
    group_width = qkv_weight.shape[2]
    width = norm_gain.shape[1]
    heads = group_width // width
    half = nz // 2
    out_cols = stale_out.shape[1]
    tiles = refresh.shape[0]
    tile_rows = rows // tiles
    weight = jnp.transpose(qkv_weight, (1, 0, 2))
    bf16, f32 = jnp.bfloat16, jnp.float32
    dma = pltpu.SemaphoreType.DMA
    vmem = pl.BlockSpec(memory_space=pltpu.VMEM)
    anywhere = pl.BlockSpec(memory_space=pltpu.HBM)
    return pl.pallas_call(
        functools.partial(kernel, nx, nz),
        out_shape=pltpu.VMEM((rows, out_cols), bf16),
        in_specs=[anywhere] * 7,
        out_specs=vmem,
        scratch_shapes=[
            pltpu.VMEM(image_tokens.shape, bf16),
            pltpu.SMEM(refresh.shape, jnp.int32),
            pltpu.VMEM(norm_gain.shape, f32),
            pltpu.VMEM(stale_kv.shape, bf16),
            pltpu.VMEM(stale_out.shape, bf16),
            pltpu.VMEM((heads, model_width, 2 * width), bf16),
            pltpu.VMEM((model_width, group_width), bf16),
            pltpu.VMEM((heads, 3, rows, width), bf16),
            pltpu.VMEM((heads, 2, 4 * half, rows, width), bf16),
            pltpu.VMEM((heads, nx, rows, width), bf16),
            pltpu.VMEM((heads, width, nx * rows), f32),
            pltpu.VMEM((heads, 8, nx * rows), f32),
            pltpu.VMEM((heads, nx - 1, tiles, width, tile_rows), bf16),
            pltpu.VMEM((heads, nx - 1, tiles, width, tile_rows), bf16),
            pltpu.VMEM((heads, nx - 1, 8, rows), f32),
            pltpu.VMEM((heads, tiles, width, tile_rows), bf16),
            pltpu.VMEM((heads, tiles, 4, width, tile_rows), bf16),
            pltpu.VMEM((heads, 4, width, out_cols), bf16),
            dma((2 * heads + 6,)), dma,
            dma((heads, 3)), dma((heads, 3)),
            dma((heads, nx - 1)), dma((heads, nx - 1)),
            dma((heads, half, 2, 2)), dma((heads, half, 2, 2)),
            dma((heads, half + 1)), dma((heads, half + 1)),
            dma((3,)), dma((3,)),
            dma((heads, nx - 1, tiles + 1)), dma((heads, nx - 1, tiles + 1)),
            dma((heads, tiles, 4)), dma((heads, tiles, 4)),
        ],
        compiler_params=pltpu.CompilerParams(
            collective_id=0, has_side_effects=True, vmem_limit_bytes=56 << 20
        ),
    )(
        *(
            pltpu.with_memory_space_constraint(array, pltpu.HBM)
            for array in (
                image_tokens, refresh, weight, norm_gain, stale_kv,
                out_weight.reshape(heads, width, out_weight.shape[1]), stale_out,
            )
        )
    )


def solution(mesh, nx=4, nz=8):
    placed = (
        P("patch", None),
        P("patch"),
        P(None, None, "head"),
        P(),
        P("patch", None, "head"),
        P("head", None),
        P("patch", "head"),
    )
    return jax.shard_map(
        functools.partial(local, nx, nz),
        mesh=mesh, in_specs=placed, out_specs=P("patch", "head"), check_vma=False,
    )
```

```python
import functools
import math

import jax
import jax.numpy as jnp
from jax import lax
from jax.experimental import pallas as pl
from jax.experimental.pallas import tpu as pltpu
from jax.sharding import PartitionSpec as P

MESH = pl.DeviceIdType.MESH
ROWS_BY_ROWS = (((1,), (1,)), ((), ()))
COLUMNS_BY_COLUMNS = (((0,), (0,)), ((), ()))


def kernel(
    nx, nz,
    tokens_far, refresh_far, qkv_weight, gain_far, stale_kv_far, out_weight, stale_out_far,
    out,
    tokens, refresh, gain, stale_kv, stale_out,
    kv_weight, q_weight, stage, kv_buf, q_buf, acc, den,
    num_stage, num_in, den_in, att_stage, att_all, out_weight_all,
    load_sem,
    swap_s, swap_r, x_s, x_r, z_s, z_r, sib_s, sib_r, w_s, w_r, num_s, num_r, den_s, den_r, att_s, att_r,
):
    heads, _, rows, width = stage.shape
    half = nz // 2
    out_cols = stale_out.shape[1]
    tiles = refresh.shape[0]
    tile_rows = rows // tiles
    patch, head = lax.axis_index("patch"), lax.axis_index("head")
    x, yh, z = patch // (2 * nz), (patch // nz) % 2, patch % nz
    yl, core = head // 2, head % 2

    def device(x_to, yh_to, z_to, yl_to, core_to):
        return ((x_to * 2 + yh_to) * nz + z_to, yl_to * 2 + core_to)

    sibling = device(x, yh, z, yl, 1 - core)
    swapped = device(x, core, z, 1 - yl, yh)
    along_z = (
        device(x, yh, (z + 1) % nz, yl, core),
        device(x, yh, (z + nz - 1) % nz, yl, core),
    )

    def along_x(step):
        return device((x + step) % nx, yh, z, yl, core)

    def send(src, dst, send_sem, recv_sem, to):
        return pltpu.make_async_remote_copy(
            src_ref=src, dst_ref=dst, send_sem=send_sem, recv_sem=recv_sem,
            device_id=to, device_id_type=MESH,
        )

    def load_kv_weight(h, j):
        return pltpu.make_async_copy(
            qkv_weight.at[1 + j, :, pl.ds(h * width, width)],
            kv_weight.at[h, :, pl.ds(j * width, width)],
            load_sem.at[0 if h == 0 else h],
        )

    def load(far, near, index):
        return pltpu.make_async_copy(far, near, load_sem.at[heads + index])

    def halves(i):
        return pl.ds(i * (tokens.shape[1] // 2), tokens.shape[1] // 2)

    def load_tokens(i):
        return load(tokens_far.at[:, halves(i)], tokens.at[:, halves(i)], 5 + i)

    def load_first(i):
        return load(
            qkv_weight.at[1, halves(i), pl.ds(0, width)], kv_weight.at[0, halves(i), pl.ds(0, width)], 7 + i
        )

    load_refresh = load(refresh_far, refresh, 1)
    load_gain = load(gain_far, gain, 2)
    load_stale_kv = load(stale_kv_far, stale_kv, 3)
    load_stale_out = load(stale_out_far, stale_out, 4)
    load_q_weight = load(qkv_weight.at[0], q_weight, 0)

    def swap(h, j):
        dst = q_buf.at[h, 0] if j == 0 else kv_buf.at[h, j - 1, 0]
        return send(stage.at[h, j], dst, swap_s, swap_r.at[h, j], swapped)

    def gather_x(h, j):
        return send(q_buf.at[h, 0], q_buf.at[h, j], x_s, x_r.at[h], along_x(j))

    def spot(s, way):
        return 4 * s - 2 + way

    def move(h, way, index, src, dst):
        return send(src, dst, z_s, z_r.at[h, way, index], along_z[way])

    def ring_own(h, way, c):
        return move(h, way, c, kv_buf.at[h, c, 0], kv_buf.at[h, c, spot(1, way)])

    def ring(h, s, way, c):
        return move(h, way, 2 * s + c, kv_buf.at[h, c, spot(s, way)], kv_buf.at[h, c, spot(s + 1, way)])

    def ring_last(h, way):
        s = half - 1
        return move(h, way, 2 * s, kv_buf.at[h, way, spot(s, way)], kv_buf.at[h, way, 4 * half - 2])

    def landed(h, s, way, c):
        here = kv_buf.at[h, c, spot(s, way)]
        return move(h, way, 2 * (s - 1) + c, here, here)

    def share(h, s, first, count):
        return send(
            kv_buf.at[h, :, pl.ds(first, count)], kv_buf.at[h, :, pl.ds(first + count, count)],
            sib_s, sib_r.at[h, s], sibling,
        )

    def share_own(h):
        return share(h, 0, 0, 1)

    def share_step(h, s):
        return share(h, s, 4 * s - 2, 2)

    def share_last(h):
        return share(h, half, 4 * half - 2, 1)

    group = yl * 2 + core
    cross_yh = (yh + core) % 2

    def weight_columns(block):
        return out_weight.at[:, :, pl.ds(pl.multiple_of(block * out_cols, out_cols), out_cols)]

    def weight_own():
        return pltpu.make_async_copy(weight_columns(group), out_weight_all.at[:, group], w_r)

    def weight_sibling(slot):
        return send(
            weight_columns(yl * 2 + 1 - core), out_weight_all.at[:, slot],
            w_s, w_r, sibling,
        )

    def weight_cross(c, slot):
        return send(
            weight_columns((1 - yl) * 2 + c), out_weight_all.at[:, slot],
            w_s, w_r, device(x, cross_yh, z, 1 - yl, c),
        )

    def sum_num(h, j, i):
        return send(
            num_stage.at[h, j - 1, i], num_in.at[h, j - 1, i],
            num_s, num_r.at[h, i], along_x(nx - j),
        )

    def sum_den(h, j):
        return send(
            den.at[h, :, pl.ds(j * rows, rows)], den_in.at[h, j - 1],
            den_s, den_r.at[h], along_x(nx - j),
        )

    held_group = (1 - yl) * 2 + yh

    def hand_out(h, i, d, slot):
        return send(
            att_stage.at[h, i], att_all.at[h, i, slot],
            att_s, att_r.at[h, i], device(x, core, z, d // 2, d % 2),
        )

    def keep(h, i):
        return pltpu.make_async_copy(att_stage.at[h, i], att_all.at[h, i, held_group], att_r.at[h, i])

    def arrived(ref, sem):
        pltpu.make_async_copy(ref, ref, sem).wait()

    def left(ref, sem):
        send(ref, ref, sem, sib_r.at[0, 0], sibling).wait_send()

    def compute(h, first, count, fresh):
        keys = kv_buf[h, 0, pl.ds(first, count)].reshape(count * rows, width)
        values = kv_buf[h, 1, pl.ds(first, count)].reshape(count * rows, width)
        scores = lax.dot_general(
            keys, q_buf[h].reshape(nx * rows, width), ROWS_BY_ROWS, preferred_element_type=jnp.float32
        )
        weights = jnp.exp2(scores)
        part = jnp.sum(weights.reshape(count * rows // 8, 8, nx * rows), axis=0)
        product = lax.dot_general(
            values, weights.astype(jnp.bfloat16), COLUMNS_BY_COLUMNS, preferred_element_type=jnp.float32
        )
        if fresh:
            acc[h], den[h] = product, part
        else:
            acc[h] += product
            den[h] += part

    def marked(i, shape):
        return jnp.broadcast_to(refresh[i], shape) > 0

    def normed(part, row):
        mean_square = jnp.mean(part * part, axis=-1, keepdims=True)
        return part * lax.rsqrt(mean_square + 1e-06) * row

    for copy in (load_stale_kv, load_gain, load_refresh):
        copy.start()
    for i in range(2):
        load_tokens(i).start()
        load_first(i).start()
    load_kv_weight(0, 1).start()

    barrier = pltpu.get_barrier_semaphore()
    peers = [along_x(j) for j in range(1, nx)] + list(along_z)
    for other in range(1, 8):
        bits = (other // 4, (other // 2) % 2, other % 2)
        peers.append(device(x, (yh + bits[0]) % 2, z, (yl + bits[1]) % 2, (core + bits[2]) % 2))
    for peer in peers:
        pl.semaphore_signal(barrier, inc=1, device_id=peer, device_id_type=MESH)

    for copy in (load_stale_kv, load_gain, load_refresh):
        copy.wait()
    scale = math.log2(math.e) / math.sqrt(width)
    query_gain = gain[pl.ds(0, 1), :] * scale
    key_gain = gain[pl.ds(1, 1), :]

    def kept(h):
        return stale_kv[:, :, h * width : (h + 1) * width].astype(jnp.float32)

    def place(h, j, fresh, stale):
        for i in range(tiles):
            span = slice(i * tile_rows, (i + 1) * tile_rows)
            old = stale[span, j, :]
            stage[h, 1 + j, span] = jnp.where(marked(i, old.shape), fresh[span], old).astype(jnp.bfloat16)
        if h == 0 and j == 0:
            pl.semaphore_wait(barrier, len(peers))
        swap(h, 1 + j).start()

    def project(h, columns):
        return jnp.dot(tokens[...], kv_weight[h, :, columns], preferred_element_type=jnp.float32)

    stale = kept(0)
    fresh = None
    for i in range(2):
        load_tokens(i).wait()
        load_first(i).wait()
        if i == 1:
            for h in range(1, heads):
                for j in range(2):
                    load_kv_weight(h, j).start()
            load_q_weight.start()
            load_stale_out.start()
        part = jnp.dot(
            tokens[:, halves(i)], kv_weight[0, halves(i), pl.ds(0, width)], preferred_element_type=jnp.float32
        )
        fresh = part if i == 0 else fresh + part
    place(0, 0, normed(fresh, key_gain), stale)
    load_kv_weight(0, 1).wait()
    place(0, 1, project(0, slice(width, 2 * width)), stale)
    for h in range(1, heads):
        arrived(kv_weight.at[h], load_sem.at[h])
        fresh = project(h, slice(0, 2 * width))
        stale = kept(h)
        place(h, 0, normed(fresh[:, :width], key_gain), stale)
        place(h, 1, fresh[:, width:], stale)

    load_q_weight.wait()
    fresh = jnp.dot(tokens[...], q_weight[...], preferred_element_type=jnp.float32)
    for h in range(heads):
        stage[h, 0] = normed(fresh[:, h * width : (h + 1) * width], query_gain).astype(jnp.bfloat16)
        swap(h, 0).start()

    def distribute_kv(h, carry):
        for c in range(2):
            swap(h, 1 + c).wait_recv()
            for way in range(2):
                ring_own(h, way, c).start()
        share_own(h).start()
        return carry

    def distribute_q(h, carry):
        swap(h, 0).wait_recv()
        for j in range(1, nx):
            gather_x(h, j).start()
        return carry

    lax.fori_loop(0, heads, distribute_kv, 0)
    lax.fori_loop(0, heads, distribute_q, 0)
    weight_own().start()
    weight_sibling(group).start()
    for c in range(2):
        weight_cross(c, group).start()

    order = sorted(
        ((h, s) for h in range(heads) for s in range(1, half + 1)),
        key=lambda pair: (pair[0] + 2 * pair[1], pair[0]),
    )

    def look_up(i):
        h, s = order[0]
        for place, (h_there, s_there) in enumerate(order):
            h = jnp.where(i == place, h_there, h)
            s = jnp.where(i == place, s_there, s)
        return h, s

    def arrive(h, s):
        @pl.when(s < half - 1)
        def _():
            for turned in range(2):
                for way in range(2):
                    c = (way + turned) % 2
                    landed(h, s, way, c).wait_recv()
                    if turned == 0:
                        ring(h, s, way, c).start()
                    else:

                        @pl.when(jnp.logical_or(h < heads - 1, s < half - 2))
                        def _(way=way, c=c):
                            ring(h, s, way, c).start()

        @pl.when(s == half - 1)
        def _():
            for way in range(2):
                landed(h, s, way, way).wait_recv()
                ring_last(h, way).start()

            @pl.when(h == heads - 2)
            def _():
                for way in range(2):
                    ring(heads - 1, half - 2, way, 1 - way).start()

            for way in range(2):
                landed(h, s, way, 1 - way).wait_recv()

        @pl.when(s < half)
        def _():
            share_step(h, s).start()

        @pl.when(s == half)
        def _():
            for way in range(2):
                ring_last(h, way).wait_recv()
            share_last(h).start()

    def work(h, s):
        @pl.when(s == 1)
        def _():
            arrived(q_buf.at[h, pl.ds(1, nx - 1)], x_r.at[h])
            share_own(h).wait_recv()
            compute(h, 0, 2, True)

        share_step(h, s).wait_recv()
        compute(h, 4 * s - 2, 4, False)

    def work_last(h):
        share_last(h).wait_recv()
        compute(h, 4 * half - 2, 2, False)
        for j in range(1, nx):
            sum_den(h, j).start()
        for i in range(tiles):
            for j in range(1, nx):
                first = j * rows + i * tile_rows
                num_stage[h, j - 1, i] = acc[h, :, first : first + tile_rows].astype(jnp.bfloat16)
                sum_num(h, j, i).start()

    def turn(i, carry):
        arrive(*look_up(i))

        @pl.when(i > 0)
        def _():
            work(*look_up(i - 1))

        return carry

    lax.fori_loop(0, len(order) - 3, turn, 0)
    last = heads - 1
    for way in range(2):
        landed(last, half - 1, way, way).wait_recv()
        ring_last(last, way).start()

    def close(i, carry):
        h = heads - 3 + i

        @pl.when(i == 1)
        def _():
            for way in range(2):
                landed(last, half - 1, way, 1 - way).wait_recv()
            share_step(last, half - 1).start()

        @pl.when(i == 2)
        def _():
            work(last, half - 1)

        work_last(h)

        @pl.when(i < 2)
        def _():
            for way in range(2):
                ring_last(h + 1, way).wait_recv()
            share_last(h + 1).start()

        return carry

    lax.fori_loop(0, 3, close, 0)

    arrived(out_weight_all, w_r)
    load_stale_out.wait()

    def attended(h, carry):
        denominator = den[h, :, :rows]
        arrived(den_in.at[h], den_r.at[h])
        for j in range(1, nx):
            denominator += den_in[h, j - 1]
        denominator = jnp.sum(denominator, axis=0, keepdims=True)
        for i in range(tiles):
            span = slice(i * tile_rows, (i + 1) * tile_rows)
            numerator = acc[h, :, span]
            arrived(num_in.at[h, :, i], num_r.at[h, i])
            for j in range(1, nx):
                numerator += num_in[h, j - 1, i].astype(jnp.float32)
            result = (numerator / denominator[:, span]).astype(jnp.bfloat16)
            att_stage[h, i] = result
            for d in range(4):

                @pl.when(jnp.logical_or(yh != core, head != d))
                def _(d=d, i=i):
                    hand_out(h, i, d, held_group).start()

            @pl.when(yh == core)
            def _(i=i):
                keep(h, i).start()

        return carry

    lax.fori_loop(0, heads, attended, 0)

    total = [None] * tiles
    for h in range(heads):
        for i in range(tiles):
            arrived(att_all.at[h, i], att_r.at[h, i])
            part = lax.dot_general(
                att_all[h, i].reshape(4 * width, tile_rows),
                out_weight_all[h].reshape(4 * width, out_cols),
                COLUMNS_BY_COLUMNS,
                preferred_element_type=jnp.float32,
            )
            total[i] = part if h == 0 else total[i] + part
            if h == heads - 1:
                span = slice(i * tile_rows, (i + 1) * tile_rows)
                stale = stale_out[span].astype(jnp.float32)
                out[span] = jnp.where(marked(i, stale.shape), total[i], stale).astype(jnp.bfloat16)

    left(stage, swap_s)
    left(q_buf.at[:, pl.ds(0, nx - 1)], x_s)
    left(kv_buf.at[:, :, pl.ds(0, 2 * half - 1)], z_s)
    left(kv_buf.at[:, :, pl.ds(0, 2 * half)], sib_s)
    left(out_weight_all.at[:, pl.ds(0, 3)], w_s)
    left(num_stage, num_s)
    left(den_in, den_s)

    @pl.when(yh == core)
    def _():
        left(att_all.at[:, :, pl.ds(0, 3)], att_s)

    @pl.when(yh != core)
    def _():
        left(att_all, att_s)


def local(nx, nz, image_tokens, refresh, qkv_weight, norm_gain, stale_kv, out_weight, stale_out):
    rows, model_width = image_tokens.shape
    group_width = qkv_weight.shape[2]
    width = norm_gain.shape[1]
    heads = group_width // width
    half = nz // 2
    out_cols = stale_out.shape[1]
    tiles = refresh.shape[0]
    tile_rows = rows // tiles
    weight = jnp.transpose(qkv_weight, (1, 0, 2))
    bf16, f32 = jnp.bfloat16, jnp.float32
    dma = pltpu.SemaphoreType.DMA
    vmem = pl.BlockSpec(memory_space=pltpu.VMEM)
    anywhere = pl.BlockSpec(memory_space=pltpu.HBM)
    return pl.pallas_call(
        functools.partial(kernel, nx, nz),
        out_shape=pltpu.VMEM((rows, out_cols), bf16),
        in_specs=[anywhere] * 7,
        out_specs=vmem,
        scratch_shapes=[
            pltpu.VMEM(image_tokens.shape, bf16),
            pltpu.SMEM(refresh.shape, jnp.int32),
            pltpu.VMEM(norm_gain.shape, f32),
            pltpu.VMEM(stale_kv.shape, bf16),
            pltpu.VMEM(stale_out.shape, bf16),
            pltpu.VMEM((heads, model_width, 2 * width), bf16),
            pltpu.VMEM((model_width, group_width), bf16),
            pltpu.VMEM((heads, 3, rows, width), bf16),
            pltpu.VMEM((heads, 2, 4 * half, rows, width), bf16),
            pltpu.VMEM((heads, nx, rows, width), bf16),
            pltpu.VMEM((heads, width, nx * rows), f32),
            pltpu.VMEM((heads, 8, nx * rows), f32),
            pltpu.VMEM((heads, nx - 1, tiles, width, tile_rows), bf16),
            pltpu.VMEM((heads, nx - 1, tiles, width, tile_rows), bf16),
            pltpu.VMEM((heads, nx - 1, 8, rows), f32),
            pltpu.VMEM((heads, tiles, width, tile_rows), bf16),
            pltpu.VMEM((heads, tiles, 4, width, tile_rows), bf16),
            pltpu.VMEM((heads, 4, width, out_cols), bf16),
            dma((heads + 9,)),
            dma, dma((heads, 3)),
            dma, dma((heads,)),
            dma, dma((heads, 2, 2 * half - 1)),
            dma, dma((heads, half + 1)),
            dma, dma,
            dma, dma((heads, tiles)),
            dma, dma((heads,)),
            dma, dma((heads, tiles)),
        ],
        compiler_params=pltpu.CompilerParams(
            collective_id=0, has_side_effects=True, vmem_limit_bytes=56 << 20
        ),
    )(
        *(
            pltpu.with_memory_space_constraint(array, pltpu.HBM)
            for array in (
                image_tokens, refresh, weight, norm_gain, stale_kv,
                out_weight.reshape(heads, width, out_weight.shape[1]), stale_out,
            )
        )
    )


def solution(mesh, nx=4, nz=8):
    placed = (
        P("patch", None),
        P("patch"),
        P(None, None, "head"),
        P(),
        P("patch", None, "head"),
        P("head", None),
        P("patch", "head"),
    )
    return jax.shard_map(
        functools.partial(local, nx, nz),
        mesh=mesh, in_specs=placed, out_specs=P("patch", "head"), check_vma=False,
    )
```

```python
import functools
import math

import jax
import jax.numpy as jnp
from jax import lax
from jax.experimental import pallas as pl
from jax.experimental.pallas import tpu as pltpu
from jax.sharding import PartitionSpec as P

MESH = pl.DeviceIdType.MESH
ROWS_BY_ROWS = (((1,), (1,)), ((), ()))
COLUMNS_BY_COLUMNS = (((0,), (0,)), ((), ()))


def kernel(
    nx, nz,
    tokens_far, refresh_far, qkv_weight, gain_far, stale_kv_far, out_weight, stale_out_far,
    out,
    tokens, refresh, gain, stale_kv, stale_out,
    kv_weight, q_weight, stage, kv_buf, q_buf, acc, den,
    num_stage, num_in, den_in, att_stage, att_all, out_weight_all,
    load_sem,
    swap_s, swap_r, x_s, x_r, z_s, z_r, sib_s, sib_r, w_s, w_r, num_s, num_r, den_s, den_r, att_s, att_r,
):
    heads, _, rows, width = stage.shape
    half = nz // 2
    out_cols = stale_out.shape[1]
    tiles = refresh.shape[0]
    tile_rows = rows // tiles
    patch, head = lax.axis_index("patch"), lax.axis_index("head")
    x, yh, z = patch // (2 * nz), (patch // nz) % 2, patch % nz
    yl, core = head // 2, head % 2

    far_first = sorted(range(1, nx), key=lambda step: -min(step, nx - step))

    def device(x_to, yh_to, z_to, yl_to, core_to):
        return ((x_to * 2 + yh_to) * nz + z_to, yl_to * 2 + core_to)

    sibling = device(x, yh, z, yl, 1 - core)
    swapped = device(x, core, z, yl, yh)
    moves = yh != core
    along_z = (
        device(x, yh, (z + 1) % nz, yl, core),
        device(x, yh, (z + nz - 1) % nz, yl, core),
    )

    def along_x(step):
        return device((x + step) % nx, yh, z, yl, core)

    def send(src, dst, send_sem, recv_sem, to):
        return pltpu.make_async_remote_copy(
            src_ref=src, dst_ref=dst, send_sem=send_sem, recv_sem=recv_sem,
            device_id=to, device_id_type=MESH,
        )

    def load_kv_weight(h, j):
        return pltpu.make_async_copy(
            qkv_weight.at[1 + j, :, pl.ds(h * width, width)],
            kv_weight.at[h, :, pl.ds(j * width, width)],
            load_sem.at[0 if h == 0 else h],
        )

    def load(far, near, index):
        return pltpu.make_async_copy(far, near, load_sem.at[heads + index])

    def halves(i):
        return pl.ds(i * (tokens.shape[1] // 2), tokens.shape[1] // 2)

    def load_tokens(i):
        return load(tokens_far.at[:, halves(i)], tokens.at[:, halves(i)], 5 + i)

    def load_first(i):
        return load(
            qkv_weight.at[1, halves(i), pl.ds(0, width)], kv_weight.at[0, halves(i), pl.ds(0, width)], 7 + i
        )

    load_refresh = load(refresh_far, refresh, 1)
    load_gain = load(gain_far, gain, 2)
    load_stale_kv = load(stale_kv_far, stale_kv, 3)
    load_stale_out = load(stale_out_far, stale_out, 4)
    load_q_weight = load(qkv_weight.at[0], q_weight, 0)

    def swap(h, j):
        dst = q_buf.at[h, 0] if j == 0 else kv_buf.at[h, j - 1, 0]
        return send(stage.at[h, j], dst, swap_s, swap_r.at[h, j], swapped)

    def gather_x(h, j):
        return send(q_buf.at[h, 0], q_buf.at[h, j], x_s, x_r.at[h], along_x(j))

    def spot(s, way):
        return 4 * s - 2 + way

    def move(h, way, index, src, dst):
        return send(src, dst, z_s, z_r.at[h, way, index], along_z[way])

    def ring_own(h, way, c):
        return move(h, way, c, kv_buf.at[h, c, 0], kv_buf.at[h, c, spot(1, way)])

    def ring(h, s, way, c):
        return move(h, way, 2 * s + c, kv_buf.at[h, c, spot(s, way)], kv_buf.at[h, c, spot(s + 1, way)])

    def ring_last(h, way):
        s = half - 1
        return move(h, way, 2 * s, kv_buf.at[h, way, spot(s, way)], kv_buf.at[h, way, 4 * half - 2])

    def landed(h, s, way, c):
        here = kv_buf.at[h, c, spot(s, way)]
        return move(h, way, 2 * (s - 1) + c, here, here)

    def share(h, s, first, count):
        return send(
            kv_buf.at[h, :, pl.ds(first, count)], kv_buf.at[h, :, pl.ds(first + count, count)],
            sib_s, sib_r.at[h, s], sibling,
        )

    def share_own(h):
        return share(h, 0, 0, 1)

    def share_step(h, s):
        return share(h, s, 4 * s - 2, 2)

    def share_last(h):
        return share(h, half, 4 * half - 2, 1)

    group = yl * 2 + core
    cross_yh = (yh + core) % 2

    def weight_columns(block):
        return out_weight.at[:, :, pl.ds(pl.multiple_of(block * out_cols, out_cols), out_cols)]

    def weight_own():
        return pltpu.make_async_copy(weight_columns(group), out_weight_all.at[:, group], w_r)

    def weight_sibling(slot):
        return send(
            weight_columns(yl * 2 + 1 - core), out_weight_all.at[:, slot],
            w_s, w_r, sibling,
        )

    def weight_cross(c, slot):
        return send(
            weight_columns((1 - yl) * 2 + c), out_weight_all.at[:, slot],
            w_s, w_r, device(x, cross_yh, z, 1 - yl, c),
        )

    def sum_num(h, j, i):
        return send(
            num_stage.at[h, j - 1, i], num_in.at[h, j - 1, i],
            num_s, num_r.at[h, i], along_x(nx - j),
        )

    def sum_den(h, j):
        return send(
            den.at[h, :, pl.ds(j * rows, rows)], den_in.at[h, j - 1],
            den_s, den_r.at[h], along_x(nx - j),
        )

    held_group = yl * 2 + yh

    def hand_out(h, i, d, slot):
        return send(
            att_stage.at[h, i], att_all.at[h, i, slot],
            att_s, att_r.at[h, i], device(x, core, z, d // 2, d % 2),
        )

    def keep(h, i):
        return pltpu.make_async_copy(att_stage.at[h, i], att_all.at[h, i, held_group], att_r.at[h, i])

    def arrived(ref, sem):
        pltpu.make_async_copy(ref, ref, sem).wait()

    def left(ref, sem):
        send(ref, ref, sem, sib_r.at[0, 0], sibling).wait_send()

    def compute(h, first, count, fresh):
        keys = kv_buf[h, 0, pl.ds(first, count)].reshape(count * rows, width)
        values = kv_buf[h, 1, pl.ds(first, count)].reshape(count * rows, width)
        scores = lax.dot_general(
            keys, q_buf[h].reshape(nx * rows, width), ROWS_BY_ROWS, preferred_element_type=jnp.float32
        )
        weights = jnp.exp2(scores)
        part = jnp.sum(weights.reshape(count * rows // 8, 8, nx * rows), axis=0)
        product = lax.dot_general(
            values, weights.astype(jnp.bfloat16), COLUMNS_BY_COLUMNS, preferred_element_type=jnp.float32
        )
        if fresh:
            acc[h], den[h] = product, part
        else:
            acc[h] += product
            den[h] += part

    def marked(i, shape):
        return jnp.broadcast_to(refresh[i], shape) > 0

    def normed(part, row):
        mean_square = jnp.mean(part * part, axis=-1, keepdims=True)
        return part * lax.rsqrt(mean_square + 1e-06) * row

    for copy in (load_stale_kv, load_gain, load_refresh):
        copy.start()
    for i in range(2):
        load_tokens(i).start()
        load_first(i).start()
    load_kv_weight(0, 1).start()

    barrier = pltpu.get_barrier_semaphore()
    peers = [along_x(j) for j in range(1, nx)] + list(along_z)
    for other in range(1, 8):
        bits = (other // 4, (other // 2) % 2, other % 2)
        peers.append(device(x, (yh + bits[0]) % 2, z, (yl + bits[1]) % 2, (core + bits[2]) % 2))
    for peer in peers:
        pl.semaphore_signal(barrier, inc=1, device_id=peer, device_id_type=MESH)

    for copy in (load_stale_kv, load_gain, load_refresh):
        copy.wait()
    scale = math.log2(math.e) / math.sqrt(width)
    query_gain = gain[pl.ds(0, 1), :] * scale
    key_gain = gain[pl.ds(1, 1), :]

    def kept(h):
        return stale_kv[:, :, h * width : (h + 1) * width].astype(jnp.float32)

    def place(h, j, fresh, stale):
        for i in range(tiles):
            span = slice(i * tile_rows, (i + 1) * tile_rows)
            old = stale[span, j, :]
            new = jnp.where(marked(i, old.shape), fresh[span], old).astype(jnp.bfloat16)

            @pl.when(moves)
            def _(span=span, new=new):
                stage[h, 1 + j, span] = new

            @pl.when(jnp.logical_not(moves))
            def _(span=span, new=new):
                kv_buf[h, j, 0, span] = new

        if h == 0 and j == 0:
            pl.semaphore_wait(barrier, len(peers))

        @pl.when(moves)
        def _():
            swap(h, 1 + j).start()

        @pl.when(jnp.logical_not(moves))
        def _():
            for way in range(2):
                ring_own(h, way, j).start()

    def project(h, columns):
        return jnp.dot(tokens[...], kv_weight[h, :, columns], preferred_element_type=jnp.float32)

    stale = kept(0)
    fresh = None
    for i in range(2):
        load_tokens(i).wait()
        load_first(i).wait()
        if i == 1:
            for h in range(1, heads):
                for j in range(2):
                    load_kv_weight(h, j).start()
            load_q_weight.start()
            load_stale_out.start()
        part = jnp.dot(
            tokens[:, halves(i)], kv_weight[0, halves(i), pl.ds(0, width)], preferred_element_type=jnp.float32
        )
        fresh = part if i == 0 else fresh + part
    place(0, 0, normed(fresh, key_gain), stale)
    load_kv_weight(0, 1).wait()
    place(0, 1, project(0, slice(width, 2 * width)), stale)
    for h in range(1, heads):
        arrived(kv_weight.at[h], load_sem.at[h])
        fresh = project(h, slice(0, 2 * width))
        stale = kept(h)
        place(h, 0, normed(fresh[:, :width], key_gain), stale)
        place(h, 1, fresh[:, width:], stale)

    load_q_weight.wait()
    fresh = jnp.dot(tokens[...], q_weight[...], preferred_element_type=jnp.float32)
    for h in range(heads):
        query = normed(fresh[:, h * width : (h + 1) * width], query_gain).astype(jnp.bfloat16)

        @pl.when(moves)
        def _(h=h, query=query):
            stage[h, 0] = query
            swap(h, 0).start()

        @pl.when(jnp.logical_not(moves))
        def _(h=h, query=query):
            q_buf[h, 0] = query
            for j in far_first:
                gather_x(h, j).start()

    def distribute_kv(h, carry):
        @pl.when(moves)
        def _():
            for c in range(2):
                swap(h, 1 + c).wait_recv()
                for way in range(2):
                    ring_own(h, way, c).start()

        share_own(h).start()
        return carry

    def distribute_q(h, carry):
        @pl.when(moves)
        def _():
            swap(h, 0).wait_recv()
            for j in far_first:
                gather_x(h, j).start()

        return carry

    lax.fori_loop(0, heads, distribute_kv, 0)
    lax.fori_loop(0, heads, distribute_q, 0)
    weight_own().start()
    weight_sibling(group).start()
    for c in range(2):
        weight_cross(c, group).start()

    order = sorted(
        ((h, s) for h in range(heads) for s in range(1, half + 1)),
        key=lambda pair: (pair[0] + 2 * pair[1], pair[0]),
    )

    def look_up(i):
        h, s = order[0]
        for place, (h_there, s_there) in enumerate(order):
            h = jnp.where(i == place, h_there, h)
            s = jnp.where(i == place, s_there, s)
        return h, s

    def arrive(h, s):
        @pl.when(s < half - 1)
        def _():
            for turned in range(2):
                for way in range(2):
                    c = (way + turned) % 2
                    landed(h, s, way, c).wait_recv()
                    if turned == 0:
                        ring(h, s, way, c).start()
                    else:

                        @pl.when(jnp.logical_or(h < heads - 1, s < half - 2))
                        def _(way=way, c=c):
                            ring(h, s, way, c).start()

        @pl.when(s == half - 1)
        def _():
            for way in range(2):
                landed(h, s, way, way).wait_recv()
                ring_last(h, way).start()

            @pl.when(h == heads - 2)
            def _():
                for way in range(2):
                    ring(heads - 1, half - 2, way, 1 - way).start()

            for way in range(2):
                landed(h, s, way, 1 - way).wait_recv()

        @pl.when(s < half)
        def _():
            share_step(h, s).start()

        @pl.when(s == half)
        def _():
            for way in range(2):
                ring_last(h, way).wait_recv()
            share_last(h).start()

    def work(h, s):
        @pl.when(s == 1)
        def _():
            arrived(q_buf.at[h, pl.ds(1, nx - 1)], x_r.at[h])
            share_own(h).wait_recv()
            compute(h, 0, 2, True)

        share_step(h, s).wait_recv()
        compute(h, 4 * s - 2, 4, False)

    def work_last(h):
        share_last(h).wait_recv()
        compute(h, 4 * half - 2, 2, False)
        for j in far_first:
            sum_den(h, j).start()
        for i in range(tiles):
            for j in far_first:
                first = j * rows + i * tile_rows
                num_stage[h, j - 1, i] = acc[h, :, first : first + tile_rows].astype(jnp.bfloat16)
                sum_num(h, j, i).start()

    def turn(i, carry):
        arrive(*look_up(i))

        @pl.when(i > 0)
        def _():
            work(*look_up(i - 1))

        return carry

    lax.fori_loop(0, len(order) - 3, turn, 0)
    last = heads - 1
    for way in range(2):
        landed(last, half - 1, way, way).wait_recv()
        ring_last(last, way).start()

    def close(i, carry):
        h = heads - 3 + i

        @pl.when(i == 1)
        def _():
            for way in range(2):
                landed(last, half - 1, way, 1 - way).wait_recv()
            share_step(last, half - 1).start()

        @pl.when(i == 2)
        def _():
            work(last, half - 1)

        work_last(h)

        @pl.when(i < 2)
        def _():
            for way in range(2):
                ring_last(h + 1, way).wait_recv()
            share_last(h + 1).start()

        return carry

    lax.fori_loop(0, 3, close, 0)

    arrived(out_weight_all, w_r)
    load_stale_out.wait()

    def attended(h, carry):
        denominator = den[h, :, :rows]
        arrived(den_in.at[h], den_r.at[h])
        for j in range(1, nx):
            denominator += den_in[h, j - 1]
        denominator = jnp.sum(denominator, axis=0, keepdims=True)
        for i in range(tiles):
            span = slice(i * tile_rows, (i + 1) * tile_rows)
            numerator = acc[h, :, span]
            arrived(num_in.at[h, :, i], num_r.at[h, i])
            for j in range(1, nx):
                numerator += num_in[h, j - 1, i].astype(jnp.float32)
            result = (numerator / denominator[:, span]).astype(jnp.bfloat16)
            att_stage[h, i] = result
            for near in range(4):
                d = (near // 2 + yl) % 2 * 2 + near % 2

                @pl.when(jnp.logical_or(yh != core, head != d))
                def _(d=d, i=i):
                    hand_out(h, i, d, held_group).start()

            @pl.when(yh == core)
            def _(i=i):
                keep(h, i).start()

        return carry

    lax.fori_loop(0, heads, attended, 0)

    total = [None] * tiles
    for h in range(heads):
        for i in range(tiles):
            arrived(att_all.at[h, i], att_r.at[h, i])
            part = lax.dot_general(
                att_all[h, i].reshape(4 * width, tile_rows),
                out_weight_all[h].reshape(4 * width, out_cols),
                COLUMNS_BY_COLUMNS,
                preferred_element_type=jnp.float32,
            )
            total[i] = part if h == 0 else total[i] + part
            if h == heads - 1:
                span = slice(i * tile_rows, (i + 1) * tile_rows)
                stale = stale_out[span].astype(jnp.float32)
                out[span] = jnp.where(marked(i, stale.shape), total[i], stale).astype(jnp.bfloat16)


    @pl.when(moves)
    def _():
        left(stage, swap_s)

    left(q_buf.at[:, pl.ds(0, nx - 1)], x_s)
    left(kv_buf.at[:, :, pl.ds(0, 2 * half - 1)], z_s)
    left(kv_buf.at[:, :, pl.ds(0, 2 * half)], sib_s)
    left(out_weight_all.at[:, pl.ds(0, 3)], w_s)
    left(num_stage, num_s)
    left(den_in, den_s)

    @pl.when(yh == core)
    def _():
        left(att_all.at[:, :, pl.ds(0, 3)], att_s)

    @pl.when(yh != core)
    def _():
        left(att_all, att_s)


def local(nx, nz, image_tokens, refresh, qkv_weight, norm_gain, stale_kv, out_weight, stale_out):
    rows, model_width = image_tokens.shape
    group_width = qkv_weight.shape[2]
    width = norm_gain.shape[1]
    heads = group_width // width
    half = nz // 2
    out_cols = stale_out.shape[1]
    tiles = refresh.shape[0]
    tile_rows = rows // tiles
    weight = jnp.transpose(qkv_weight, (1, 0, 2))
    bf16, f32 = jnp.bfloat16, jnp.float32
    dma = pltpu.SemaphoreType.DMA
    vmem = pl.BlockSpec(memory_space=pltpu.VMEM)
    anywhere = pl.BlockSpec(memory_space=pltpu.HBM)
    return pl.pallas_call(
        functools.partial(kernel, nx, nz),
        out_shape=pltpu.VMEM((rows, out_cols), bf16),
        in_specs=[anywhere] * 7,
        out_specs=vmem,
        scratch_shapes=[
            pltpu.VMEM(image_tokens.shape, bf16),
            pltpu.SMEM(refresh.shape, jnp.int32),
            pltpu.VMEM(norm_gain.shape, f32),
            pltpu.VMEM(stale_kv.shape, bf16),
            pltpu.VMEM(stale_out.shape, bf16),
            pltpu.VMEM((heads, model_width, 2 * width), bf16),
            pltpu.VMEM((model_width, group_width), bf16),
            pltpu.VMEM((heads, 3, rows, width), bf16),
            pltpu.VMEM((heads, 2, 4 * half, rows, width), bf16),
            pltpu.VMEM((heads, nx, rows, width), bf16),
            pltpu.VMEM((heads, width, nx * rows), f32),
            pltpu.VMEM((heads, 8, nx * rows), f32),
            pltpu.VMEM((heads, nx - 1, tiles, width, tile_rows), bf16),
            pltpu.VMEM((heads, nx - 1, tiles, width, tile_rows), bf16),
            pltpu.VMEM((heads, nx - 1, 8, rows), f32),
            pltpu.VMEM((heads, tiles, width, tile_rows), bf16),
            pltpu.VMEM((heads, tiles, 4, width, tile_rows), bf16),
            pltpu.VMEM((heads, 4, width, out_cols), bf16),
            dma((heads + 9,)),
            dma, dma((heads, 3)),
            dma, dma((heads,)),
            dma, dma((heads, 2, 2 * half - 1)),
            dma, dma((heads, half + 1)),
            dma, dma,
            dma, dma((heads, tiles)),
            dma, dma((heads,)),
            dma, dma((heads, tiles)),
        ],
        compiler_params=pltpu.CompilerParams(
            collective_id=0, has_side_effects=True, vmem_limit_bytes=56 << 20
        ),
    )(
        *(
            pltpu.with_memory_space_constraint(array, pltpu.HBM)
            for array in (
                image_tokens, refresh, weight, norm_gain, stale_kv,
                out_weight.reshape(heads, width, out_weight.shape[1]), stale_out,
            )
        )
    )


def solution(mesh, nx=4, nz=8):
    placed = (
        P("patch", None),
        P("patch"),
        P(None, None, "head"),
        P(),
        P("patch", None, "head"),
        P("head", None),
        P("patch", "head"),
    )
    return jax.shard_map(
        functools.partial(local, nx, nz),
        mesh=mesh, in_specs=placed, out_specs=P("patch", "head"), check_vma=False,
    )
```

```python
import functools
import math

import jax
import jax.numpy as jnp
from jax import lax
from jax.experimental import pallas as pl
from jax.experimental.pallas import tpu as pltpu
from jax.sharding import PartitionSpec as P

MESH = pl.DeviceIdType.MESH
ROWS_BY_ROWS = (((1,), (1,)), ((), ()))
COLUMNS_BY_COLUMNS = (((0,), (0,)), ((), ()))


def kernel(
    nx, nz,
    tokens_far, refresh_far, qkv_weight, gain_far, stale_kv_far, out_weight, stale_out_far,
    out,
    tokens, refresh, gain, stale_kv, stale_out,
    kv_weight, q_weight, stage, kv_buf, q_buf, acc, den,
    num_stage, num_in, den_in, att_stage, att_all, out_weight_all,
    load_sem,
    swap_s, swap_r, x_s, x_r, z_s, z_r, sib_s, sib_r, w_s, w_r, num_s, num_r, den_s, den_r, att_s, att_r,
):
    heads, _, rows, width = stage.shape
    half = nz // 2
    out_cols = stale_out.shape[1]
    tiles = refresh.shape[0]
    tile_rows = rows // tiles
    patch, head = lax.axis_index("patch"), lax.axis_index("head")
    x, yh, z = patch // (2 * nz), (patch // nz) % 2, patch % nz
    yl, core = head // 2, head % 2

    far_first = sorted(range(1, nx), key=lambda step: -min(step, nx - step))

    def device(x_to, yh_to, z_to, yl_to, core_to):
        return ((x_to * 2 + yh_to) * nz + z_to, yl_to * 2 + core_to)

    sibling = device(x, yh, z, yl, 1 - core)
    swapped = device(x, core, z, yl, yh)
    moves = yh != core
    along_z = (
        device(x, yh, (z + 1) % nz, yl, core),
        device(x, yh, (z + nz - 1) % nz, yl, core),
    )

    def along_x(step):
        return device((x + step) % nx, yh, z, yl, core)

    def send(src, dst, send_sem, recv_sem, to):
        return pltpu.make_async_remote_copy(
            src_ref=src, dst_ref=dst, send_sem=send_sem, recv_sem=recv_sem,
            device_id=to, device_id_type=MESH,
        )

    def load_kv_weight(h, j):
        return pltpu.make_async_copy(
            qkv_weight.at[1 + j, :, pl.ds(h * width, width)],
            kv_weight.at[h, :, pl.ds(j * width, width)],
            load_sem.at[0 if h == 0 else h],
        )

    def load(far, near, index):
        return pltpu.make_async_copy(far, near, load_sem.at[heads + index])

    def halves(i):
        return pl.ds(i * (tokens.shape[1] // 2), tokens.shape[1] // 2)

    def load_tokens(i):
        return load(tokens_far.at[:, halves(i)], tokens.at[:, halves(i)], 5 + i)

    def load_first(i):
        return load(
            qkv_weight.at[1, halves(i), pl.ds(0, width)], kv_weight.at[0, halves(i), pl.ds(0, width)], 7 + i
        )

    load_refresh = load(refresh_far, refresh, 1)
    load_gain = load(gain_far, gain, 2)
    load_stale_kv = load(stale_kv_far, stale_kv, 3)
    load_stale_out = load(stale_out_far, stale_out, 4)
    load_q_weight = load(qkv_weight.at[0], q_weight, 0)

    def swap(h, j):
        dst = q_buf.at[h, 0] if j == 0 else kv_buf.at[h, j - 1, 0]
        return send(stage.at[h, j], dst, swap_s, swap_r.at[h, j], swapped)

    def gather_x(h, j):
        return send(q_buf.at[h, 0], q_buf.at[h, j], x_s, x_r.at[h], along_x(j))

    def spot(s, way):
        return 4 * s - 2 + way

    def move(h, way, index, src, dst):
        return send(src, dst, z_s, z_r.at[h, way, index], along_z[way])

    def ring_own(h, way, c):
        return move(h, way, c, kv_buf.at[h, c, 0], kv_buf.at[h, c, spot(1, way)])

    def ring(h, s, way, c):
        return move(h, way, 2 * s + c, kv_buf.at[h, c, spot(s, way)], kv_buf.at[h, c, spot(s + 1, way)])

    def ring_last(h, way):
        s = half - 1
        return move(h, way, 2 * s, kv_buf.at[h, way, spot(s, way)], kv_buf.at[h, way, 4 * half - 2])

    def landed(h, s, way, c):
        here = kv_buf.at[h, c, spot(s, way)]
        return move(h, way, 2 * (s - 1) + c, here, here)

    def share(h, s, first, count):
        return send(
            kv_buf.at[h, :, pl.ds(first, count)], kv_buf.at[h, :, pl.ds(first + count, count)],
            sib_s, sib_r.at[h, s], sibling,
        )

    def share_own(h):
        return share(h, 0, 0, 1)

    def share_step(h, s):
        return share(h, s, 4 * s - 2, 2)

    def share_last(h):
        return share(h, half, 4 * half - 2, 1)

    group = yl * 2 + core
    cross_yh = (yh + core) % 2

    def weight_columns(block):
        return out_weight.at[:, :, pl.ds(pl.multiple_of(block * out_cols, out_cols), out_cols)]

    def weight_own():
        return pltpu.make_async_copy(weight_columns(group), out_weight_all.at[:, group], w_r)

    def weight_sibling(slot):
        return send(
            weight_columns(yl * 2 + 1 - core), out_weight_all.at[:, slot],
            w_s, w_r, sibling,
        )

    def weight_cross(c, slot):
        return send(
            weight_columns((1 - yl) * 2 + c), out_weight_all.at[:, slot],
            w_s, w_r, device(x, cross_yh, z, 1 - yl, c),
        )

    def sum_num(h, j, i):
        return send(
            num_stage.at[h, j - 1, i], num_in.at[h, j - 1, i],
            num_s, num_r.at[h, i], along_x(nx - j),
        )

    def sum_den(h, j):
        return send(
            den.at[h, :, pl.ds(j * rows, rows)], den_in.at[h, j - 1],
            den_s, den_r.at[h], along_x(nx - j),
        )

    held_group = yl * 2 + yh

    def hand_out(h, i, d, slot):
        return send(
            att_stage.at[h, i], att_all.at[h, i, slot],
            att_s, att_r.at[h, i], device(x, core, z, d // 2, d % 2),
        )

    def keep(h, i):
        return pltpu.make_async_copy(att_stage.at[h, i], att_all.at[h, i, held_group], att_r.at[h, i])

    def arrived(ref, sem):
        pltpu.make_async_copy(ref, ref, sem).wait()

    def left(ref, sem):
        send(ref, ref, sem, sib_r.at[0, 0], sibling).wait_send()

    def compute(h, first, count, fresh):
        keys = kv_buf[h, 0, pl.ds(first, count)].reshape(count * rows, width)
        values = kv_buf[h, 1, pl.ds(first, count)].reshape(count * rows, width)
        scores = lax.dot_general(
            keys, q_buf[h].reshape(nx * rows, width), ROWS_BY_ROWS, preferred_element_type=jnp.float32
        )
        weights = jnp.exp2(scores)
        part = jnp.sum(weights.reshape(count * rows // 8, 8, nx * rows), axis=0)
        product = lax.dot_general(
            values, weights.astype(jnp.bfloat16), COLUMNS_BY_COLUMNS, preferred_element_type=jnp.float32
        )
        if fresh:
            acc[h], den[h] = product, part
        else:
            acc[h] += product
            den[h] += part

    def marked(i, shape):
        return jnp.broadcast_to(refresh[i], shape) > 0

    def normed(part, row):
        mean_square = jnp.mean(part * part, axis=-1, keepdims=True)
        return part * lax.rsqrt(mean_square + 1e-06) * row

    for copy in (load_stale_kv, load_gain, load_refresh):
        copy.start()
    for i in range(2):
        load_tokens(i).start()
        load_first(i).start()
    load_kv_weight(0, 1).start()

    barrier = pltpu.get_barrier_semaphore()
    peers = [along_x(j) for j in range(1, nx)] + list(along_z)
    for other in range(1, 8):
        bits = (other // 4, (other // 2) % 2, other % 2)
        peers.append(device(x, (yh + bits[0]) % 2, z, (yl + bits[1]) % 2, (core + bits[2]) % 2))
    for peer in peers:
        pl.semaphore_signal(barrier, inc=1, device_id=peer, device_id_type=MESH)

    for copy in (load_stale_kv, load_gain, load_refresh):
        copy.wait()
    scale = math.log2(math.e) / math.sqrt(width)
    query_gain = gain[pl.ds(0, 1), :] * scale
    key_gain = gain[pl.ds(1, 1), :]

    def kept(h):
        return stale_kv[:, :, h * width : (h + 1) * width].astype(jnp.float32)

    def place(h, j, fresh, stale):
        for i in range(tiles):
            span = slice(i * tile_rows, (i + 1) * tile_rows)
            old = stale[span, j, :]
            new = jnp.where(marked(i, old.shape), fresh[span], old).astype(jnp.bfloat16)

            @pl.when(moves)
            def _(span=span, new=new):
                stage[h, 1 + j, span] = new

            @pl.when(jnp.logical_not(moves))
            def _(span=span, new=new):
                kv_buf[h, j, 0, span] = new

        if h == 0 and j == 0:
            pl.semaphore_wait(barrier, len(peers))

        @pl.when(moves)
        def _():
            swap(h, 1 + j).start()

        @pl.when(jnp.logical_not(moves))
        def _():
            for way in range(2):
                ring_own(h, way, j).start()

    def project(h, columns):
        return jnp.dot(tokens[...], kv_weight[h, :, columns], preferred_element_type=jnp.float32)

    stale = kept(0)
    fresh = None
    for i in range(2):
        load_tokens(i).wait()
        load_first(i).wait()
        if i == 1:
            for h in range(1, heads):
                for j in range(2):
                    load_kv_weight(h, j).start()
            load_q_weight.start()
            load_stale_out.start()
        part = jnp.dot(
            tokens[:, halves(i)], kv_weight[0, halves(i), pl.ds(0, width)], preferred_element_type=jnp.float32
        )
        fresh = part if i == 0 else fresh + part
    place(0, 0, normed(fresh, key_gain), stale)
    load_kv_weight(0, 1).wait()
    place(0, 1, project(0, slice(width, 2 * width)), stale)
    for h in range(1, heads):
        arrived(kv_weight.at[h], load_sem.at[h])
        fresh = project(h, slice(0, 2 * width))
        stale = kept(h)
        place(h, 0, normed(fresh[:, :width], key_gain), stale)
        place(h, 1, fresh[:, width:], stale)

    load_q_weight.wait()
    fresh = jnp.dot(tokens[...], q_weight[...], preferred_element_type=jnp.float32)
    for h in range(heads):
        query = normed(fresh[:, h * width : (h + 1) * width], query_gain).astype(jnp.bfloat16)

        @pl.when(moves)
        def _(h=h, query=query):
            stage[h, 0] = query
            swap(h, 0).start()

        @pl.when(jnp.logical_not(moves))
        def _(h=h, query=query):
            q_buf[h, 0] = query
            for j in far_first:
                gather_x(h, j).start()

    def distribute_kv(h, carry):
        @pl.when(moves)
        def _():
            for c in range(2):
                swap(h, 1 + c).wait_recv()
                for way in range(2):
                    ring_own(h, way, c).start()

        share_own(h).start()
        return carry

    def distribute_q(h, carry):
        @pl.when(moves)
        def _():
            swap(h, 0).wait_recv()
            for j in far_first:
                gather_x(h, j).start()

        return carry

    lax.fori_loop(0, heads, distribute_kv, 0)
    lax.fori_loop(0, heads, distribute_q, 0)
    weight_own().start()
    weight_sibling(group).start()
    for c in range(2):
        weight_cross(c, group).start()

    order = sorted(
        ((h, s) for h in range(heads) for s in range(1, half + 1)),
        key=lambda pair: (pair[0] + 2 * pair[1], pair[0]),
    )

    def look_up(i):
        h, s = order[0]
        for place, (h_there, s_there) in enumerate(order):
            h = jnp.where(i == place, h_there, h)
            s = jnp.where(i == place, s_there, s)
        return h, s

    def arrive(h, s):
        @pl.when(s < half - 1)
        def _():
            for turned in range(2):
                for way in range(2):
                    c = (way + turned) % 2
                    landed(h, s, way, c).wait_recv()
                    if turned == 0:
                        ring(h, s, way, c).start()
                    else:

                        @pl.when(jnp.logical_or(h < heads - 1, s < half - 2))
                        def _(way=way, c=c):
                            ring(h, s, way, c).start()

        @pl.when(s == half - 1)
        def _():
            for way in range(2):
                landed(h, s, way, way).wait_recv()
                ring_last(h, way).start()

            @pl.when(h == heads - 2)
            def _():
                for way in range(2):
                    ring(heads - 1, half - 2, way, 1 - way).start()

            for way in range(2):
                landed(h, s, way, 1 - way).wait_recv()

        @pl.when(s < half)
        def _():
            share_step(h, s).start()

        @pl.when(s == half)
        def _():
            for way in range(2):
                ring_last(h, way).wait_recv()
            share_last(h).start()

    def work(h, s):
        @pl.when(s == 1)
        def _():
            arrived(q_buf.at[h, pl.ds(1, nx - 1)], x_r.at[h])
            share_own(h).wait_recv()
            share_step(h, s).wait_recv()
            compute(h, 0, 6, True)

        @pl.when(s > 1)
        def _():
            share_step(h, s).wait_recv()
            compute(h, 4 * s - 2, 4, False)

    def work_last(h):
        share_last(h).wait_recv()
        compute(h, 4 * half - 2, 2, False)
        for j in far_first:
            sum_den(h, j).start()
        for i in range(tiles):
            for j in far_first:
                first = j * rows + i * tile_rows
                num_stage[h, j - 1, i] = acc[h, :, first : first + tile_rows].astype(jnp.bfloat16)
                sum_num(h, j, i).start()

    def turn(i, carry):
        arrive(*look_up(i))

        @pl.when(i > 0)
        def _():
            work(*look_up(i - 1))

        return carry

    lax.fori_loop(0, len(order) - 3, turn, 0)
    last = heads - 1
    for way in range(2):
        landed(last, half - 1, way, way).wait_recv()
        ring_last(last, way).start()

    def close(i, carry):
        h = heads - 3 + i

        @pl.when(i == 1)
        def _():
            for way in range(2):
                landed(last, half - 1, way, 1 - way).wait_recv()
            share_step(last, half - 1).start()

        @pl.when(i == 2)
        def _():
            work(last, half - 1)

        work_last(h)

        @pl.when(i < 2)
        def _():
            for way in range(2):
                ring_last(h + 1, way).wait_recv()
            share_last(h + 1).start()

        return carry

    lax.fori_loop(0, 3, close, 0)

    arrived(out_weight_all, w_r)
    load_stale_out.wait()

    def attended(h, carry):
        denominator = den[h, :, :rows]
        arrived(den_in.at[h], den_r.at[h])
        for j in range(1, nx):
            denominator += den_in[h, j - 1]
        denominator = jnp.sum(denominator, axis=0, keepdims=True)
        for i in range(tiles):
            span = slice(i * tile_rows, (i + 1) * tile_rows)
            numerator = acc[h, :, span]
            arrived(num_in.at[h, :, i], num_r.at[h, i])
            for j in range(1, nx):
                numerator += num_in[h, j - 1, i].astype(jnp.float32)
            result = (numerator / denominator[:, span]).astype(jnp.bfloat16)
            att_stage[h, i] = result
            for near in range(4):
                d = (near // 2 + yl) % 2 * 2 + near % 2

                @pl.when(jnp.logical_or(yh != core, head != d))
                def _(d=d, i=i):
                    hand_out(h, i, d, held_group).start()

            @pl.when(yh == core)
            def _(i=i):
                keep(h, i).start()

        return carry

    lax.fori_loop(0, heads, attended, 0)

    total = [None] * tiles
    for h in range(heads):
        for i in range(tiles):
            arrived(att_all.at[h, i], att_r.at[h, i])
            part = lax.dot_general(
                att_all[h, i].reshape(4 * width, tile_rows),
                out_weight_all[h].reshape(4 * width, out_cols),
                COLUMNS_BY_COLUMNS,
                preferred_element_type=jnp.float32,
            )
            total[i] = part if h == 0 else total[i] + part
            if h == heads - 1:
                span = slice(i * tile_rows, (i + 1) * tile_rows)
                stale = stale_out[span].astype(jnp.float32)
                out[span] = jnp.where(marked(i, stale.shape), total[i], stale).astype(jnp.bfloat16)


    @pl.when(moves)
    def _():
        left(stage, swap_s)

    left(q_buf.at[:, pl.ds(0, nx - 1)], x_s)
    left(kv_buf.at[:, :, pl.ds(0, 2 * half - 1)], z_s)
    left(kv_buf.at[:, :, pl.ds(0, 2 * half)], sib_s)
    left(out_weight_all.at[:, pl.ds(0, 3)], w_s)
    left(num_stage, num_s)
    left(den_in, den_s)

    @pl.when(yh == core)
    def _():
        left(att_all.at[:, :, pl.ds(0, 3)], att_s)

    @pl.when(yh != core)
    def _():
        left(att_all, att_s)


def local(nx, nz, image_tokens, refresh, qkv_weight, norm_gain, stale_kv, out_weight, stale_out):
    rows, model_width = image_tokens.shape
    group_width = qkv_weight.shape[2]
    width = norm_gain.shape[1]
    heads = group_width // width
    half = nz // 2
    out_cols = stale_out.shape[1]
    tiles = refresh.shape[0]
    tile_rows = rows // tiles
    weight = jnp.transpose(qkv_weight, (1, 0, 2))
    bf16, f32 = jnp.bfloat16, jnp.float32
    dma = pltpu.SemaphoreType.DMA
    vmem = pl.BlockSpec(memory_space=pltpu.VMEM)
    anywhere = pl.BlockSpec(memory_space=pltpu.HBM)
    return pl.pallas_call(
        functools.partial(kernel, nx, nz),
        out_shape=pltpu.VMEM((rows, out_cols), bf16),
        in_specs=[anywhere] * 7,
        out_specs=vmem,
        scratch_shapes=[
            pltpu.VMEM(image_tokens.shape, bf16),
            pltpu.SMEM(refresh.shape, jnp.int32),
            pltpu.VMEM(norm_gain.shape, f32),
            pltpu.VMEM(stale_kv.shape, bf16),
            pltpu.VMEM(stale_out.shape, bf16),
            pltpu.VMEM((heads, model_width, 2 * width), bf16),
            pltpu.VMEM((model_width, group_width), bf16),
            pltpu.VMEM((heads, 3, rows, width), bf16),
            pltpu.VMEM((heads, 2, 4 * half, rows, width), bf16),
            pltpu.VMEM((heads, nx, rows, width), bf16),
            pltpu.VMEM((heads, width, nx * rows), f32),
            pltpu.VMEM((heads, 8, nx * rows), f32),
            pltpu.VMEM((heads, nx - 1, tiles, width, tile_rows), bf16),
            pltpu.VMEM((heads, nx - 1, tiles, width, tile_rows), bf16),
            pltpu.VMEM((heads, nx - 1, 8, rows), f32),
            pltpu.VMEM((heads, tiles, width, tile_rows), bf16),
            pltpu.VMEM((heads, tiles, 4, width, tile_rows), bf16),
            pltpu.VMEM((heads, 4, width, out_cols), bf16),
            dma((heads + 9,)),
            dma, dma((heads, 3)),
            dma, dma((heads,)),
            dma, dma((heads, 2, 2 * half - 1)),
            dma, dma((heads, half + 1)),
            dma, dma,
            dma, dma((heads, tiles)),
            dma, dma((heads,)),
            dma, dma((heads, tiles)),
        ],
        compiler_params=pltpu.CompilerParams(
            collective_id=0, has_side_effects=True, vmem_limit_bytes=56 << 20
        ),
    )(
        *(
            pltpu.with_memory_space_constraint(array, pltpu.HBM)
            for array in (
                image_tokens, refresh, weight, norm_gain, stale_kv,
                out_weight.reshape(heads, width, out_weight.shape[1]), stale_out,
            )
        )
    )


def solution(mesh, nx=4, nz=8):
    placed = (
        P("patch", None),
        P("patch"),
        P(None, None, "head"),
        P(),
        P("patch", None, "head"),
        P("head", None),
        P("patch", "head"),
    )
    return jax.shard_map(
        functools.partial(local, nx, nz),
        mesh=mesh, in_specs=placed, out_specs=P("patch", "head"), check_vma=False,
    )
```

```python
import functools
import math

import jax
import jax.numpy as jnp
from jax import lax
from jax.experimental import pallas as pl
from jax.experimental.pallas import tpu as pltpu
from jax.sharding import PartitionSpec as P

MESH = pl.DeviceIdType.MESH
ROWS_BY_ROWS = (((1,), (1,)), ((), ()))
COLUMNS_BY_COLUMNS = (((0,), (0,)), ((), ()))


def kernel(
    nx, nz,
    tokens_far, refresh_far, qkv_weight, gain_far, stale_kv_far, out_weight, stale_out_far,
    out,
    tokens, refresh, gain, stale_kv, stale_out,
    kv_weight, q_weight, stage, kv_buf, q_buf, acc, den,
    num_stage, num_in, den_in, att_stage, att_all, out_weight_all,
    load_sem,
    swap_s, swap_r, x_s, x_r, z_s, z_r, sib_s, sib_r, w_s, w_r, num_s, num_r, den_s, den_r, att_s, att_r,
):
    heads, _, rows, width = stage.shape
    half = nz // 2
    out_cols = stale_out.shape[1]
    tiles = refresh.shape[0]
    tile_rows = rows // tiles
    patch, head = lax.axis_index("patch"), lax.axis_index("head")
    x, yh, z = patch // (2 * nz), (patch // nz) % 2, patch % nz
    yl, core = head // 2, head % 2

    far_first = sorted(range(1, nx), key=lambda step: -min(step, nx - step))

    def device(x_to, yh_to, z_to, yl_to, core_to):
        return ((x_to * 2 + yh_to) * nz + z_to, yl_to * 2 + core_to)

    sibling = device(x, yh, z, yl, 1 - core)
    swapped = device(x, core, z, yl, yh)
    moves = yh != core
    along_z = (
        device(x, yh, (z + 1) % nz, yl, core),
        device(x, yh, (z + nz - 1) % nz, yl, core),
    )

    def along_x(step):
        return device((x + step) % nx, yh, z, yl, core)

    def send(src, dst, send_sem, recv_sem, to):
        return pltpu.make_async_remote_copy(
            src_ref=src, dst_ref=dst, send_sem=send_sem, recv_sem=recv_sem,
            device_id=to, device_id_type=MESH,
        )

    def load_kv_weight(h, j):
        return pltpu.make_async_copy(
            qkv_weight.at[1 + j, :, pl.ds(h * width, width)],
            kv_weight.at[h, :, pl.ds(j * width, width)],
            load_sem.at[0 if h == 0 else h],
        )

    def load(far, near, index):
        return pltpu.make_async_copy(far, near, load_sem.at[heads + index])

    def halves(i):
        return pl.ds(i * (tokens.shape[1] // 2), tokens.shape[1] // 2)

    def load_tokens(i):
        return load(tokens_far.at[:, halves(i)], tokens.at[:, halves(i)], 5 + i)

    def load_first(i):
        return load(
            qkv_weight.at[1, halves(i), pl.ds(0, width)], kv_weight.at[0, halves(i), pl.ds(0, width)], 7 + i
        )

    load_refresh = load(refresh_far, refresh, 1)
    load_gain = load(gain_far, gain, 2)
    load_stale_kv = load(stale_kv_far, stale_kv, 3)
    load_stale_out = load(stale_out_far, stale_out, 4)
    load_q_weight = load(qkv_weight.at[0], q_weight, 0)

    def swap(h, j):
        dst = q_buf.at[h, 0] if j == 0 else kv_buf.at[h, j - 1, 0]
        return send(stage.at[h, j], dst, swap_s, swap_r.at[h, j], swapped)

    def gather_x(h, j):
        return send(q_buf.at[h, 0], q_buf.at[h, j], x_s, x_r.at[h], along_x(j))

    def spot(s, way):
        return 4 * s - 2 + way

    def move(h, way, index, src, dst):
        return send(src, dst, z_s, z_r.at[h, way, index], along_z[way])

    def ring_own(h, way, c):
        return move(h, way, c, kv_buf.at[h, c, 0], kv_buf.at[h, c, spot(1, way)])

    def ring(h, s, way, c):
        return move(h, way, 2 * s + c, kv_buf.at[h, c, spot(s, way)], kv_buf.at[h, c, spot(s + 1, way)])

    def ring_last(h, way):
        s = half - 1
        return move(h, way, 2 * s, kv_buf.at[h, way, spot(s, way)], kv_buf.at[h, way, 4 * half - 2])

    def landed(h, s, way, c):
        here = kv_buf.at[h, c, spot(s, way)]
        return move(h, way, 2 * (s - 1) + c, here, here)

    def share(h, s, first, count):
        return send(
            kv_buf.at[h, :, pl.ds(first, count)], kv_buf.at[h, :, pl.ds(first + count, count)],
            sib_s, sib_r.at[h, s], sibling,
        )

    def share_own(h):
        return share(h, 0, 0, 1)

    def share_step(h, s):
        return share(h, s, 4 * s - 2, 2)

    def share_last(h):
        return share(h, half, 4 * half - 2, 1)

    group = yl * 2 + core
    cross_yh = (yh + core) % 2

    def weight_columns(block):
        return out_weight.at[:, :, pl.ds(pl.multiple_of(block * out_cols, out_cols), out_cols)]

    def weight_own():
        return pltpu.make_async_copy(weight_columns(group), out_weight_all.at[:, group], w_r)

    def weight_sibling(slot):
        return send(
            weight_columns(yl * 2 + 1 - core), out_weight_all.at[:, slot],
            w_s, w_r, sibling,
        )

    def weight_cross(c, slot):
        return send(
            weight_columns((1 - yl) * 2 + c), out_weight_all.at[:, slot],
            w_s, w_r, device(x, cross_yh, z, 1 - yl, c),
        )

    def sum_num(h, j, i):
        return send(
            num_stage.at[h, j - 1, i], num_in.at[h, j - 1, i],
            num_s, num_r.at[h, i], along_x(nx - j),
        )

    def sum_den(h, j):
        return send(
            den.at[h, :, pl.ds(j * rows, rows)], den_in.at[h, j - 1],
            den_s, den_r.at[h], along_x(nx - j),
        )

    held_group = yl * 2 + yh

    def hand_out(h, i, d, slot):
        return send(
            att_stage.at[h, i], att_all.at[h, i, slot],
            att_s, att_r.at[h, i], device(x, core, z, d // 2, d % 2),
        )

    def keep(h, i):
        return pltpu.make_async_copy(att_stage.at[h, i], att_all.at[h, i, held_group], att_r.at[h, i])

    def arrived(ref, sem):
        pltpu.make_async_copy(ref, ref, sem).wait()

    def left(ref, sem):
        send(ref, ref, sem, sib_r.at[0, 0], sibling).wait_send()

    def compute(h, first, count, fresh):
        keys = kv_buf[h, 0, pl.ds(first, count)].reshape(count * rows, width)
        values = kv_buf[h, 1, pl.ds(first, count)].reshape(count * rows, width)
        scores = lax.dot_general(
            keys, q_buf[h].reshape(nx * rows, width), ROWS_BY_ROWS, preferred_element_type=jnp.float32
        )
        weights = jnp.exp2(scores)
        part = jnp.sum(weights.reshape(count * rows // 8, 8, nx * rows), axis=0)
        product = lax.dot_general(
            values, weights.astype(jnp.bfloat16), COLUMNS_BY_COLUMNS, preferred_element_type=jnp.float32
        )
        if fresh:
            acc[h], den[h] = product, part
        else:
            acc[h] += product
            den[h] += part

    def marked(i, shape):
        return jnp.broadcast_to(refresh[i], shape) > 0

    def normed(part, row):
        mean_square = jnp.mean(part * part, axis=-1, keepdims=True)
        return part * lax.rsqrt(mean_square + 1e-06) * row

    for copy in (load_stale_kv, load_gain, load_refresh):
        copy.start()
    for i in range(2):
        load_tokens(i).start()
        load_first(i).start()
    load_kv_weight(0, 1).start()

    barrier = pltpu.get_barrier_semaphore()
    peers = [along_x(j) for j in range(1, nx)] + list(along_z)
    for other in range(1, 8):
        bits = (other // 4, (other // 2) % 2, other % 2)
        peers.append(device(x, (yh + bits[0]) % 2, z, (yl + bits[1]) % 2, (core + bits[2]) % 2))
    for peer in peers:
        pl.semaphore_signal(barrier, inc=1, device_id=peer, device_id_type=MESH)

    for copy in (load_stale_kv, load_gain, load_refresh):
        copy.wait()
    scale = math.log2(math.e) / math.sqrt(width)
    query_gain = gain[pl.ds(0, 1), :] * scale
    key_gain = gain[pl.ds(1, 1), :]

    def kept(h):
        return stale_kv[:, :, h * width : (h + 1) * width].astype(jnp.float32)

    def place(h, j, fresh, stale):
        for i in range(tiles):
            span = slice(i * tile_rows, (i + 1) * tile_rows)
            old = stale[span, j, :]
            new = jnp.where(marked(i, old.shape), fresh[span], old).astype(jnp.bfloat16)

            @pl.when(moves)
            def _(span=span, new=new):
                stage[h, 1 + j, span] = new

            @pl.when(jnp.logical_not(moves))
            def _(span=span, new=new):
                kv_buf[h, j, 0, span] = new

        if h == 0 and j == 0:
            pl.semaphore_wait(barrier, len(peers))

        @pl.when(moves)
        def _():
            swap(h, 1 + j).start()

        @pl.when(jnp.logical_not(moves))
        def _():
            for way in range(2):
                ring_own(h, way, j).start()

    def project(h, columns):
        return jnp.dot(tokens[...], kv_weight[h, :, columns], preferred_element_type=jnp.float32)

    stale = kept(0)
    fresh = None
    for i in range(2):
        load_tokens(i).wait()
        load_first(i).wait()
        if i == 1:
            for h in range(1, heads):
                for j in range(2):
                    load_kv_weight(h, j).start()
            load_q_weight.start()
            load_stale_out.start()
        part = jnp.dot(
            tokens[:, halves(i)], kv_weight[0, halves(i), pl.ds(0, width)], preferred_element_type=jnp.float32
        )
        fresh = part if i == 0 else fresh + part
    place(0, 0, normed(fresh, key_gain), stale)
    load_kv_weight(0, 1).wait()
    place(0, 1, project(0, slice(width, 2 * width)), stale)
    for h in range(1, heads):
        arrived(kv_weight.at[h], load_sem.at[h])
        fresh = project(h, slice(0, 2 * width))
        stale = kept(h)
        place(h, 0, normed(fresh[:, :width], key_gain), stale)
        place(h, 1, fresh[:, width:], stale)

    load_q_weight.wait()
    fresh = jnp.dot(tokens[...], q_weight[...], preferred_element_type=jnp.float32)
    for h in range(heads):
        query = normed(fresh[:, h * width : (h + 1) * width], query_gain).astype(jnp.bfloat16)

        @pl.when(moves)
        def _(h=h, query=query):
            stage[h, 0] = query
            swap(h, 0).start()

        @pl.when(jnp.logical_not(moves))
        def _(h=h, query=query):
            q_buf[h, 0] = query
            for j in far_first:
                gather_x(h, j).start()

    def distribute_kv(h, carry):
        @pl.when(moves)
        def _():
            for c in range(2):
                swap(h, 1 + c).wait_recv()
                for way in range(2):
                    ring_own(h, way, c).start()

        share_own(h).start()
        return carry

    def distribute_q(h, carry):
        @pl.when(moves)
        def _():
            swap(h, 0).wait_recv()
            for j in far_first:
                gather_x(h, j).start()

        return carry

    lax.fori_loop(0, heads, distribute_kv, 0)
    lax.fori_loop(0, heads, distribute_q, 0)

    order = sorted(
        ((h, s) for h in range(heads) for s in range(1, half + 1)),
        key=lambda pair: (pair[0] + 2 * pair[1], pair[0]),
    )

    def look_up(i):
        h, s = order[0]
        for place, (h_there, s_there) in enumerate(order):
            h = jnp.where(i == place, h_there, h)
            s = jnp.where(i == place, s_there, s)
        return h, s

    def arrive(h, s):
        @pl.when(s < half - 1)
        def _():
            for turned in range(2):
                for way in range(2):
                    c = (way + turned) % 2
                    landed(h, s, way, c).wait_recv()
                    if turned == 0:
                        ring(h, s, way, c).start()
                    else:

                        @pl.when(jnp.logical_or(h < heads - 1, s < half - 2))
                        def _(way=way, c=c):
                            ring(h, s, way, c).start()

        @pl.when(s == half - 1)
        def _():
            for way in range(2):
                landed(h, s, way, way).wait_recv()
                ring_last(h, way).start()

            @pl.when(h == heads - 2)
            def _():
                for way in range(2):
                    ring(heads - 1, half - 2, way, 1 - way).start()

            for way in range(2):
                landed(h, s, way, 1 - way).wait_recv()

        @pl.when(s < half)
        def _():
            share_step(h, s).start()

        @pl.when(s == half)
        def _():
            for way in range(2):
                ring_last(h, way).wait_recv()
            share_last(h).start()

    def work(h, s):
        @pl.when(s == 1)
        def _():
            arrived(q_buf.at[h, pl.ds(1, nx - 1)], x_r.at[h])
            share_own(h).wait_recv()
            share_step(h, s).wait_recv()
            compute(h, 0, 6, True)

        @pl.when(s > 1)
        def _():
            share_step(h, s).wait_recv()
            compute(h, 4 * s - 2, 4, False)

    def work_last(h):
        share_last(h).wait_recv()
        compute(h, 4 * half - 2, 2, False)
        for j in far_first:
            sum_den(h, j).start()
        for i in range(tiles):
            for j in far_first:
                first = j * rows + i * tile_rows
                num_stage[h, j - 1, i] = acc[h, :, first : first + tile_rows].astype(jnp.bfloat16)
                sum_num(h, j, i).start()

    def turn(i, carry):
        arrive(*look_up(i))

        @pl.when(i == 2)
        def _():
            weight_own().start()
            weight_sibling(group).start()
            for c in range(2):
                weight_cross(c, group).start()

        @pl.when(i > 0)
        def _():
            work(*look_up(i - 1))

        return carry

    lax.fori_loop(0, len(order) - 3, turn, 0)
    last = heads - 1
    for way in range(2):
        landed(last, half - 1, way, way).wait_recv()
        ring_last(last, way).start()

    def close(i, carry):
        h = heads - 3 + i

        @pl.when(i == 1)
        def _():
            for way in range(2):
                landed(last, half - 1, way, 1 - way).wait_recv()
            share_step(last, half - 1).start()

        @pl.when(i == 2)
        def _():
            work(last, half - 1)

        work_last(h)

        @pl.when(i < 2)
        def _():
            for way in range(2):
                ring_last(h + 1, way).wait_recv()
            share_last(h + 1).start()

        return carry

    lax.fori_loop(0, 3, close, 0)

    arrived(out_weight_all, w_r)
    load_stale_out.wait()

    def attended(h, carry):
        denominator = den[h, :, :rows]
        arrived(den_in.at[h], den_r.at[h])
        for j in range(1, nx):
            denominator += den_in[h, j - 1]
        denominator = jnp.sum(denominator, axis=0, keepdims=True)
        for i in range(tiles):
            span = slice(i * tile_rows, (i + 1) * tile_rows)
            numerator = acc[h, :, span]
            arrived(num_in.at[h, :, i], num_r.at[h, i])
            for j in range(1, nx):
                numerator += num_in[h, j - 1, i].astype(jnp.float32)
            result = (numerator / denominator[:, span]).astype(jnp.bfloat16)
            att_stage[h, i] = result
            for near in range(4):
                d = (near // 2 + yl) % 2 * 2 + near % 2

                @pl.when(jnp.logical_or(yh != core, head != d))
                def _(d=d, i=i):
                    hand_out(h, i, d, held_group).start()

            @pl.when(yh == core)
            def _(i=i):
                keep(h, i).start()

        return carry

    lax.fori_loop(0, heads, attended, 0)

    total = [None] * tiles
    for h in range(heads):
        for i in range(tiles):
            arrived(att_all.at[h, i], att_r.at[h, i])
            part = lax.dot_general(
                att_all[h, i].reshape(4 * width, tile_rows),
                out_weight_all[h].reshape(4 * width, out_cols),
                COLUMNS_BY_COLUMNS,
                preferred_element_type=jnp.float32,
            )
            total[i] = part if h == 0 else total[i] + part
            if h == heads - 1:
                span = slice(i * tile_rows, (i + 1) * tile_rows)
                stale = stale_out[span].astype(jnp.float32)
                out[span] = jnp.where(marked(i, stale.shape), total[i], stale).astype(jnp.bfloat16)


    @pl.when(moves)
    def _():
        left(stage, swap_s)

    left(q_buf.at[:, pl.ds(0, nx - 1)], x_s)
    left(kv_buf.at[:, :, pl.ds(0, 2 * half - 1)], z_s)
    left(kv_buf.at[:, :, pl.ds(0, 2 * half)], sib_s)
    left(out_weight_all.at[:, pl.ds(0, 3)], w_s)
    left(num_stage, num_s)
    left(den_in, den_s)

    @pl.when(yh == core)
    def _():
        left(att_all.at[:, :, pl.ds(0, 3)], att_s)

    @pl.when(yh != core)
    def _():
        left(att_all, att_s)


def local(nx, nz, image_tokens, refresh, qkv_weight, norm_gain, stale_kv, out_weight, stale_out):
    rows, model_width = image_tokens.shape
    group_width = qkv_weight.shape[2]
    width = norm_gain.shape[1]
    heads = group_width // width
    half = nz // 2
    out_cols = stale_out.shape[1]
    tiles = refresh.shape[0]
    tile_rows = rows // tiles
    weight = jnp.transpose(qkv_weight, (1, 0, 2))
    bf16, f32 = jnp.bfloat16, jnp.float32
    dma = pltpu.SemaphoreType.DMA
    vmem = pl.BlockSpec(memory_space=pltpu.VMEM)
    anywhere = pl.BlockSpec(memory_space=pltpu.HBM)
    return pl.pallas_call(
        functools.partial(kernel, nx, nz),
        out_shape=pltpu.VMEM((rows, out_cols), bf16),
        in_specs=[anywhere] * 7,
        out_specs=vmem,
        scratch_shapes=[
            pltpu.VMEM(image_tokens.shape, bf16),
            pltpu.SMEM(refresh.shape, jnp.int32),
            pltpu.VMEM(norm_gain.shape, f32),
            pltpu.VMEM(stale_kv.shape, bf16),
            pltpu.VMEM(stale_out.shape, bf16),
            pltpu.VMEM((heads, model_width, 2 * width), bf16),
            pltpu.VMEM((model_width, group_width), bf16),
            pltpu.VMEM((heads, 3, rows, width), bf16),
            pltpu.VMEM((heads, 2, 4 * half, rows, width), bf16),
            pltpu.VMEM((heads, nx, rows, width), bf16),
            pltpu.VMEM((heads, width, nx * rows), f32),
            pltpu.VMEM((heads, 8, nx * rows), f32),
            pltpu.VMEM((heads, nx - 1, tiles, width, tile_rows), bf16),
            pltpu.VMEM((heads, nx - 1, tiles, width, tile_rows), bf16),
            pltpu.VMEM((heads, nx - 1, 8, rows), f32),
            pltpu.VMEM((heads, tiles, width, tile_rows), bf16),
            pltpu.VMEM((heads, tiles, 4, width, tile_rows), bf16),
            pltpu.VMEM((heads, 4, width, out_cols), bf16),
            dma((heads + 9,)),
            dma, dma((heads, 3)),
            dma, dma((heads,)),
            dma, dma((heads, 2, 2 * half - 1)),
            dma, dma((heads, half + 1)),
            dma, dma,
            dma, dma((heads, tiles)),
            dma, dma((heads,)),
            dma, dma((heads, tiles)),
        ],
        compiler_params=pltpu.CompilerParams(
            collective_id=0, has_side_effects=True, vmem_limit_bytes=56 << 20
        ),
    )(
        *(
            pltpu.with_memory_space_constraint(array, pltpu.HBM)
            for array in (
                image_tokens, refresh, weight, norm_gain, stale_kv,
                out_weight.reshape(heads, width, out_weight.shape[1]), stale_out,
            )
        )
    )


def solution(mesh, nx=4, nz=8):
    placed = (
        P("patch", None),
        P("patch"),
        P(None, None, "head"),
        P(),
        P("patch", None, "head"),
        P("head", None),
        P("patch", "head"),
    )
    return jax.shard_map(
        functools.partial(local, nx, nz),
        mesh=mesh, in_specs=placed, out_specs=P("patch", "head"), check_vma=False,
    )
```
